256 devices in a mesh: pool: 32 (over z, x_lo, core), head: 8 (over y, x_hi).
Axes of the slice: x: 4 (x_hi: 2, x_lo: 2; x = x_hi * 2 + x_lo), y: 4, z: 8, core: 2. Of those that a mesh axis runs over, the one named last changes fastest.
Arguments:
- span_cache: bfloat16 [1024, 64, 576], P('pool'), may hold values from -6 to 6
- destination: int32 [1024, 1], P('pool'), may hold values from 0 to 31, as said below
- resident: bfloat16 [1536, 64, 576], P('pool'), may hold values from -6 to 6
- block_table: int32 [512, 32], P('pool'), may hold values from 0 to 111
- lengths: int32 [512], P('pool'), may hold values from 1 to 2048, as said below
- new_latent: bfloat16 [512, 4, 576], P('pool')
- query: bfloat16 [512, 4, 128, 192], P('pool', None, 'head')
- w_uk: bfloat16 [128, 128, 512], P('head'), may hold values from -0.5 to 0.5
- w_uv: bfloat16 [128, 512, 128], P('head'), may hold values from -0.25 to 0.25
- w_out: bfloat16 [16384, 7168], P('head', 'pool'), may hold values from -0.046875 to 0.046875
Outputs:
- layer_out: bfloat16 [512, 4, 7168], P('head', None, 'pool')
The draws below stay inside these ranges and needn't reach their ends.
Inputs may be any that keep to these rules, and one draw needn't show every extreme that they name: Among the 32 blocks of one source, every destination that is named is named exactly 2 times. Every row's first lengths // 64 table entries and the partial one are read; some row has the largest length in every draw.
All inputs are finite; a program needn't handle non-finite values.
Results may differ from the reference program's by a relative error of at most 0.0076.
Values may be sent and summed in bfloat16 or wider, within the bound.
A program may use at most 192 MiB of HBM per device.

```python
import jax
import jax.numpy as jnp
from jax import lax

D = 7168
HEADS = 128
RANK = 512
NOPE = 128
VDIM = 128
LAT = 576
QK = 192
BLOCK = 64
STEPS = 4
ROWS_DEV = 16
ROWS = 512
MAXBLK = 32
RES = 48
SPAN_BLK = 32
SEND_MOST = 2
PAGES_ALL = 112
N_POOL = 32


def draw_destination(key, part):
    key = jax.random.fold_in(key, 19)
    key_perm, key_sign = jax.random.split(key, 2)
    perm_keys = jax.random.split(key_perm, N_POOL)
    orders = jax.vmap(lambda one_key: jax.random.permutation(one_key, SPAN_BLK))(perm_keys).astype(jnp.int32)
    turning = jax.random.randint(key_sign, (N_POOL, 1), 0, 2) * 2 - 1
    source = jnp.arange(N_POOL, dtype=jnp.int32)[:, None]
    group = orders // SEND_MOST
    offset = jnp.where(group == 0, N_POOL // 2, jnp.where(group == 1, 1, N_POOL // 2 + turning * (group - 1)))
    dest_dev = (source + offset) % N_POOL
    return dest_dev.reshape(N_POOL * SPAN_BLK, 1).astype(jnp.int32)


def draw_block_table(key, part):
    key = jax.random.fold_in(key, 23)
    table = jax.random.randint(key, (ROWS, MAXBLK), 0, PAGES_ALL)
    row_ids = jnp.arange(ROWS, dtype=jnp.int32)
    owner_dev = row_ids // ROWS_DEV
    far_page = RES + (owner_dev + N_POOL // 2) % N_POOL * SEND_MOST
    near_page = RES + (owner_dev + N_POOL - 1) % N_POOL * SEND_MOST
    local_row = row_ids % ROWS_DEV
    first_col = jnp.where(local_row == 0, far_page, jnp.where(local_row == 1, near_page, table[:, 0]))
    table = table.at[:, 0].set(first_col)
    return table.astype(jnp.int32)


def draw_lengths(key, part):
    key = jax.random.fold_in(key, 11)
    key_raw, key_factor, key_full = jax.random.split(key, 3)
    longest = MAXBLK * BLOCK
    raw_len = jax.random.randint(key_raw, (N_POOL, ROWS_DEV), 0, longest)
    factor = jax.random.randint(key_factor, (N_POOL, 1), 1, 5)
    length_rows = jnp.minimum(1 + raw_len * factor // 4, longest).reshape(ROWS)
    chosen = jax.random.randint(key_full, (), 0, ROWS)
    return jnp.where(jnp.arange(ROWS) == chosen, longest, length_rows).astype(jnp.int32)


def draw_new_latent(key, part):
    key = jax.random.fold_in(key, 13)
    values = jax.random.normal(key, (ROWS, STEPS, LAT), jnp.float32)
    return values.astype(jnp.bfloat16)


def draw_query(key, part):
    key = jax.random.fold_in(key, 17)
    values = jax.random.normal(key, (ROWS, STEPS, HEADS, QK), jnp.float32)
    return values.astype(jnp.bfloat16)


def shard_levels(rng, extent, cuts, least, top_value):
    factor_of = 1.0
    for axis_at, parts in cuts:
        heights = jax.random.uniform(jax.random.fold_in(jax.random.fold_in(rng, 6), axis_at), (parts,), jnp.float32, least / len(cuts), top_value / len(cuts))
        factor_of = factor_of * jnp.repeat(jnp.exp(heights), extent[axis_at] // parts).reshape((-1,) + (1,) * (len(extent) - 1 - axis_at))
    return factor_of


def noise(stream_key, dims, scale, reach, cuts=(), held_as=jnp.bfloat16):
    drawn = jax.random.normal(stream_key, dims, jnp.float32) * scale
    if len(cuts) > 0:
        drawn = shard_levels(stream_key, dims, cuts, -0.22, 0.18) * drawn
    return jnp.clip(drawn, min=-reach, max=reach).astype(held_as)


def setup_inputs(seed: int = 0) -> dict:
    seeds = jax.random.split(jax.random.key(seed), 11)
    return {
        "span_cache": noise(seeds[0], (N_POOL * SPAN_BLK, BLOCK, LAT), 1.0, 6.0, ((0, 32),)),
        "destination": draw_destination(jax.random.fold_in(seeds[10], 71), 0),
        "resident": noise(seeds[2], (N_POOL * RES, BLOCK, LAT), 1.0, 6.0, ((0, 32),)),
        "block_table": draw_block_table(jax.random.fold_in(seeds[10], 71), 0),
        "lengths": draw_lengths(jax.random.fold_in(seeds[10], 71), 0),
        "new_latent": draw_new_latent(jax.random.fold_in(seeds[10], 71), 0),
        "query": draw_query(jax.random.fold_in(seeds[10], 71), 0),
        "w_uk": noise(seeds[7], (HEADS, NOPE, RANK), NOPE ** -0.5, 0.5, ((0, 8),)),
        "w_uv": noise(seeds[8], (HEADS, RANK, VDIM), RANK ** -0.5, 0.25, ((0, 8),)),
        "w_out": noise(seeds[9], (HEADS * VDIM, D), (HEADS * VDIM) ** -0.5, 0.046875, ((0, 8), (1, 32))),
    }


def reference(span_cache, destination, resident, block_table, lengths, new_latent, query, w_uk, w_uv, w_out):
    dest_dev = destination[:, 0].reshape(N_POOL, SPAN_BLK)
    onehot = (dest_dev[:, :, None] == jnp.arange(N_POOL, dtype=jnp.int32)[None, None, :]).astype(jnp.int32)
    arrival_rank = jnp.sum((jnp.cumsum(onehot, axis=1) - onehot) * onehot, axis=2)
    source = jnp.arange(N_POOL, dtype=jnp.int32)[:, None]
    target = (dest_dev * PAGES_ALL + RES + source * SEND_MOST + arrival_rank).reshape(-1).astype(jnp.int32)
    empty_pages = jnp.zeros((N_POOL, PAGES_ALL - RES, BLOCK, LAT), resident.dtype)
    page_pool = jnp.concatenate([resident.reshape(N_POOL, RES, BLOCK, LAT), empty_pages], axis=1)
    page_pool = page_pool.reshape(N_POOL * PAGES_ALL, BLOCK, LAT).at[target].set(span_cache)
    softmax_scale = QK ** -0.5
    positions = jnp.arange(MAXBLK * BLOCK, dtype=jnp.int32)
    causal = jnp.arange(STEPS)[:, None] >= jnp.arange(STEPS)[None, :]
    w_uk_full = w_uk.astype(jnp.float32)
    w_uv_full = w_uv.astype(jnp.float32)

    def one_row(row_id):
        owner_dev = row_id // ROWS_DEV
        row_table = (owner_dev * PAGES_ALL + block_table[row_id]).astype(jnp.int32)
        cached = page_pool[row_table].reshape(MAXBLK * BLOCK, LAT).astype(jnp.float32)
        fresh_lat = new_latent[row_id].astype(jnp.float32)
        query_rows = query[row_id].astype(jnp.float32)
        absorbed = jnp.einsum('thn,hnc->thc', query_rows[:, :, :NOPE], w_uk_full).astype(jnp.bfloat16)
        absorbed = lax.optimization_barrier(absorbed).astype(jnp.float32)
        query_full = jnp.concatenate([absorbed, query_rows[:, :, NOPE:]], axis=-1)
        old_scores = jnp.einsum('thc,lc->thl', query_full, cached) * softmax_scale
        old_scores = jnp.where(positions[None, None, :] < lengths[row_id], old_scores, -jnp.inf)
        new_scores = jnp.einsum('thc,sc->ths', query_full, fresh_lat) * softmax_scale
        new_scores = jnp.where(causal[:, None, :], new_scores, -jnp.inf)
        highest = jnp.maximum(jnp.max(old_scores, axis=-1), jnp.max(new_scores, axis=-1))[:, :, None]
        old_exp = jnp.exp(old_scores - highest)
        new_exp = jnp.exp(new_scores - highest)
        denominator = jnp.sum(old_exp, axis=-1, keepdims=True) + jnp.sum(new_exp, axis=-1, keepdims=True)
        old_weights = lax.optimization_barrier((old_exp / denominator).astype(jnp.bfloat16)).astype(jnp.float32)
        new_weights = lax.optimization_barrier((new_exp / denominator).astype(jnp.bfloat16)).astype(jnp.float32)
        latent_mix = jnp.einsum('thl,lc->thc', old_weights, cached[:, :RANK])
        latent_mix = latent_mix + jnp.einsum('ths,sc->thc', new_weights, fresh_lat[:, :RANK])
        latent_mix = lax.optimization_barrier(latent_mix.astype(jnp.bfloat16)).astype(jnp.float32)
        heads_out = jnp.einsum('thc,hcv->thv', latent_mix, w_uv_full).astype(jnp.bfloat16)
        return heads_out.reshape(STEPS, HEADS * VDIM)

    attended = lax.map(one_row, jnp.arange(ROWS, dtype=jnp.int32))
    layer_out = jnp.dot(attended.reshape(ROWS * STEPS, HEADS * VDIM), w_out, preferred_element_type=jnp.float32)
    return layer_out.astype(jnp.bfloat16).reshape(ROWS, STEPS, D)
```

```python
import functools

import jax
import jax.numpy as jnp
from jax import lax
from jax.experimental import pallas as pl
from jax.experimental.pallas import tpu as pltpu
from jax.sharding import PartitionSpec as P

MESH = pl.DeviceIdType.MESH
F32 = jnp.float32
BF16 = jnp.bfloat16
NT = (((1,), (1,)), ((), ()))
NN = (((1,), (0,)), ((), ()))


def coords():
    p = lax.axis_index("pool")
    h = lax.axis_index("head")
    return p // 4, lax.rem(p // 2, 2), lax.rem(p, 2), h // 2, lax.rem(h, 2)


def peer_of(e, k, z, xl, c, y, sign):
    dz = lax.rem(y + k, 4) + 4 * e
    zz = lax.rem(z + 8 + sign * dz, 8)
    return zz * 4 + lax.rem(xl + k // 2, 2) * 2 + lax.rem(c + k % 2, 2)


def attend_kernel(
    pick, q3, bias, span, resident, fresh, w_uk, w_uv, w_out,
    heads_out, wall,
    span_v, res_v, uk_v, uv_v, fresh_v, sendbuf, arr, q_abs, acc, m_s, l_s, out_v,
    load_sem, res_sem, zsend, zrecv, ysend, yrecv, wsend, wrecv, out_sem,
):
    z, xl, c, y, xh = coords()
    p = lax.axis_index("pool")
    h = lax.axis_index("head")
    g = lax.rem(p, 4)
    up = lax.rem(y + 1, 4) * 2 + xh
    down = lax.rem(y + 3, 4) * 2 + xh
    core_mate = p + 1 - 2 * c
    xl_mate = p + 2 - 4 * xl
    pairs = [(e, k) for e in range(2) for k in range(4)]

    loads = [
        pltpu.make_async_copy(span, span_v, load_sem.at[0]),
        pltpu.make_async_copy(w_uk, uk_v, load_sem.at[1]),
        pltpu.make_async_copy(fresh, fresh_v, load_sem.at[2]),
        pltpu.make_async_copy(w_uv, uv_v, load_sem.at[3]),
    ]
    res_loads = [
        pltpu.make_async_copy(resident.at[pl.ds(512 * n, 512)], res_v.at[pl.ds(512 * n, 512)], res_sem.at[n])
        for n in range(6)
    ]
    for one in loads[:3] + res_loads + loads[3:]:
        one.start()

    barrier = pltpu.get_barrier_semaphore()

    def greet(pool_to, head_to):
        pl.semaphore_signal(barrier, inc=1, device_id=(pool_to, head_to), device_id_type=MESH)

    for e, k in pairs:
        for sign in (1, -1):
            to = peer_of(e, k, z, xl, c, y, sign)
            if (e, k) == (0, 0):
                @pl.when(y != 0)
                def _(to=to):
                    greet(to, h)
            else:
                greet(to, h)
    greet(p, up)
    greet(p, down)
    greet(core_mate, h)
    greet(xl_mate, h)
    pl.semaphore_wait(barrier, 18 + 2 * jnp.where(y != 0, 1, 0))

    loads[0].wait()
    zcopies = []
    for e, k in pairs:
        i = e * 4 + k
        for ab in range(2):
            at = pick[i, ab]
            live = pick[i, 2]
            block = span_v[at] * live.astype(F32).astype(BF16)
            for slab in range(4):
                sendbuf[i, ab * 4 + slab] = block[:, slab * 128 : (slab + 1) * 128]
            if ab == 0:
                low = block[:, 512:]
            else:
                sendbuf[i, 8] = jnp.concatenate([low, block[:, 512:]], axis=1)
        to = peer_of(e, k, z, xl, c, y, 1)
        remote = pltpu.make_async_remote_copy(
            src_ref=sendbuf.at[i], dst_ref=arr.at[0, e, :, k], send_sem=zsend.at[i], recv_sem=zrecv.at[i],
            device_id=(to, h), device_id_type=MESH,
        )
        zcopies.append(remote)
        if i == 0:
            @pl.when(y != 0)
            def _(remote=remote):
                remote.start()

            @pl.when(y == 0)
            def _():
                pltpu.make_async_copy(sendbuf.at[0], arr.at[0, 0, :, 0], zrecv.at[0]).start()
        else:
            remote.start()

    def wcopy(src, owner, to, n):
        slot = lax.rem(owner - lax.rem(to, 4) + 4, 4) - 1
        return pltpu.make_async_remote_copy(
            src_ref=src, dst_ref=wall.at[slot], send_sem=wsend.at[n], recv_sem=wrecv.at[n],
            device_id=(to, h), device_id_type=MESH,
        )

    w_mate = wcopy(w_out, g, core_mate, 0)
    w_far = wcopy(w_out, g, xl_mate, 1)
    w_pass = wcopy(wall.at[1], lax.rem(g + 2, 4), core_mate, 2)
    w_mate.start()
    w_far.start()

    loads[1].wait()

    @pl.loop(0, 16)
    def _(hd):
        at = pl.ds(pl.multiple_of(hd * 64, 64), 64)
        q_abs[at, :] = jnp.dot(q3[at, :128], uk_v[hd], preferred_element_type=F32).astype(BF16)

    scale = 1.4426950408889634 * 192 ** -0.5
    TQ = 256

    def fold(at, s, values, first=False):
        top = jnp.max(s, axis=1, keepdims=True)
        if not first:
            before = m_s[at, :1]
            top = jnp.maximum(top, before)
        p_ = jnp.exp2(s - top)
        total = jnp.sum(p_, axis=1, keepdims=True)
        mix = lax.dot_general(p_.astype(BF16), values, NN, preferred_element_type=F32)
        if not first:
            fade = jnp.exp2(before - top)
            total = total + l_s[at, :1] * fade
            mix = mix + acc[at, :] * fade
        acc[at, :] = mix
        m_s[at, :] = jnp.broadcast_to(top, (TQ, 128))
        l_s[at, :] = jnp.broadcast_to(total, (TQ, 128))

    def biased(s, row):
        return (s.reshape(TQ // 16, 16, s.shape[1]) * scale + row[None]).reshape(s.shape)

    loads[2].wait()

    @pl.loop(0, 1024 // TQ)
    def _(n):
        at = pl.ds(pl.multiple_of(n * TQ, TQ), TQ)
        s = lax.dot_general(q_abs[at, :], fresh_v[:, :512], NT, preferred_element_type=F32)
        s = s + lax.dot_general(q3[at, 128:192], fresh_v[:, 512:], NT, preferred_element_type=F32)
        row = lax.broadcasted_iota(jnp.int32, s.shape, 0)
        col = lax.broadcasted_iota(jnp.int32, s.shape, 1)
        seen = ((row & 15) == (col >> 2)) & (((row >> 4) & 3) >= (col & 3))
        fold(at, jnp.where(seen, s * scale, -jnp.inf), fresh_v[:, :512], first=True)

    def resident_chunk(n):
        res_loads[n].wait()
        toks = pl.ds(512 * n, 512)

        @pl.loop(0, 1024 // TQ)
        def _(t):
            at = pl.ds(pl.multiple_of(t * TQ, TQ), TQ)
            s = lax.dot_general(q_abs[at, :], res_v[toks, :512], NT, preferred_element_type=F32)
            s = s + lax.dot_general(q3[at, 128:192], res_v[toks, 512:], NT, preferred_element_type=F32)
            fold(at, biased(s, bias[:, toks]), res_v[toks, :512])

    def arrived_chunk(rel, e):
        n = rel * 2 + e

        @pl.loop(0, 1024 // TQ)
        def _(t):
            at = pl.ds(pl.multiple_of(t * TQ, TQ), TQ)
            rope = arr[rel, e, 8].reshape(256, 128)
            parts, mains = [], []
            for ab in range(2):
                main = jnp.concatenate([arr[rel, e, ab * 4 + j].reshape(256, 128) for j in range(4)], axis=1)
                s = lax.dot_general(q_abs[at, :], main, NT, preferred_element_type=F32)
                s = s + lax.dot_general(
                    q3[at, 128 * (1 + ab) : 128 * (2 + ab)], rope, NT, preferred_element_type=F32
                )
                parts.append(s)
                mains.append(main)
            s = jnp.concatenate(parts, axis=1)
            fold(at, biased(s, bias[:, 3072 + 512 * n : 3584 + 512 * n]), jnp.concatenate(mains, axis=0))

    def ycopy(i, way, kind):
        e, k = pairs[i]
        landing = 2 if kind else (3 if way == 0 else 1)
        source = 0 if kind == 0 else (3 if way == 0 else 1)
        return pltpu.make_async_remote_copy(
            src_ref=arr.at[source, e, :, k], dst_ref=arr.at[landing, e, :, k],
            send_sem=ysend.at[way, kind, i], recv_sem=yrecv.at[way, kind, i],
            device_id=(p, up if way == 0 else down), device_id_type=MESH,
        )

    def own_step(i):
        if i == 0:
            @pl.when(y != 0)
            def _():
                zcopies[0].wait_recv()

            @pl.when(y == 0)
            def _():
                pltpu.make_async_copy(sendbuf.at[0], arr.at[0, 0, :, 0], zrecv.at[0]).wait()
        else:
            zcopies[i].wait_recv()
        ycopy(i, 0, 0).start()
        ycopy(i, 1, 0).start()

    def pass_step(i):
        ycopy(i, 0, 0).wait_recv()
        ycopy(i, 1, 0).wait_recv()
        ycopy(i, i % 4 // 2, 1).start()

    for i in range(8):
        if i < 6:
            resident_chunk(i)
        own_step(i)
        if i > 0:
            pass_step(i - 1)
        if i == 3:
            w_far.wait_recv()
            w_pass.start()
        if i == 5:
            arrived_chunk(0, 0)
        if i == 6:
            arrived_chunk(3, 0)
            arrived_chunk(1, 0)
    arrived_chunk(0, 1)
    pass_step(7)
    arrived_chunk(3, 1)
    arrived_chunk(1, 1)
    for i in range(8):
        ycopy(i, i % 4 // 2, 1).wait_recv()
        if i == 3:
            arrived_chunk(2, 0)
    arrived_chunk(2, 1)

    loads[3].wait()

    @pl.loop(0, 4)
    def _(quarter):
        for j in range(4):
            hd = quarter * 4 + j
            at = pl.ds(pl.multiple_of(hd * 64, 64), 64)
            mixed = (acc[at, :] / l_s[at, :1]).astype(BF16)
            out_v[:, pl.ds(pl.multiple_of(hd * 128, 128), 128)] = jnp.dot(
                mixed, uv_v[hd], preferred_element_type=F32
            ).astype(BF16)

    done = pltpu.make_async_copy(out_v, heads_out, out_sem)
    done.start()

    @pl.when(y != 0)
    def _():
        zcopies[0].wait_send()

    for i in range(1, 8):
        zcopies[i].wait_send()
    for i in range(8):
        ycopy(i, 0, 0).wait_send()
        ycopy(i, 1, 0).wait_send()
        ycopy(i, i % 4 // 2, 1).wait_send()
    w_mate.wait()
    w_far.wait_send()
    w_pass.wait()
    done.wait()


def project_kernel(
    heads, w_out, wall,
    out,
    w_v, hbuf, tiles, landed, load_sem, zsend, zrecv, rsend, rrecv,
):
    p = lax.axis_index("pool")
    h = lax.axis_index("head")
    z, g = p // 4, lax.rem(p, 4)
    right = lax.rem(z + 1, 8) * 4 + g
    left = lax.rem(z + 7, 8) * 4 + g

    own = pltpu.make_async_copy(heads, hbuf.at[0], load_sem.at[4])
    own.start()
    w_loads = [pltpu.make_async_copy(w_out, w_v.at[0], load_sem.at[0])] + [
        pltpu.make_async_copy(wall.at[i], w_v.at[i + 1], load_sem.at[i + 1]) for i in range(3)
    ]
    for one in w_loads:
        one.start()

    barrier = pltpu.get_barrier_semaphore()

    def greet(pool_to, head_to):
        pl.semaphore_signal(barrier, inc=1, device_id=(pool_to, head_to), device_id_type=MESH)

    greet(right, h)
    greet(left, h)
    for dh in range(8):
        for i in range(4):
            if dh or i:
                greet(z * 4 + lax.rem(g + i, 4), lax.rem(h + dh, 8))
    pl.semaphore_wait(barrier, 33)

    def zcopy(way, a, half):
        rows = pl.ds(32 * half, 32)
        src = 0 if a == 1 else 2 * (a - 1) - 1 + way
        dst = 7 if a == 4 else 2 * a - 1 + way
        return pltpu.make_async_remote_copy(
            src_ref=hbuf.at[src, rows], dst_ref=hbuf.at[dst, rows],
            send_sem=zsend.at[way, a - 1, half], recv_sem=zrecv.at[way, a - 1, half],
            device_id=(right if way == 0 else left, h), device_id_type=MESH,
        )

    own.wait()
    order = [(0, 0), (0, 1), (1, 1), (1, 0)]
    for way, half in order:
        zcopy(way, 1, half).start()

    def tile_copy(slot, i, to_head):
        return pltpu.make_async_remote_copy(
            src_ref=tiles.at[slot, i], dst_ref=landed.at[h, g],
            send_sem=rsend.at[slot, i], recv_sem=rrecv.at[h, g],
            device_id=(z * 4 + lax.rem(g + i, 4), to_head), device_id_type=MESH,
        )

    def slot_head(slot):
        if slot == 0:
            return z
        if slot == 7:
            return lax.rem(z + 4, 8)
        a = (slot + 1) // 2
        return lax.rem(z + 8 - a, 8) if slot % 2 else lax.rem(z + a, 8)

    def multiply(first, count):
        lhs = hbuf[pl.ds(first, count)].reshape(64 * count, 2048)
        for i in range(4):
            part = jnp.dot(lhs, w_v[i], preferred_element_type=F32).astype(BF16)
            for n in range(count):
                slot = first + n
                to_head = slot_head(slot)
                tiles[slot, i] = part[64 * n : 64 * (n + 1)]
                copy = tile_copy(slot, i, to_head)
                if i == 0:
                    @pl.when(to_head != h)
                    def _(copy=copy):
                        copy.start()

                    @pl.when(to_head == h)
                    def _(slot=slot):
                        landed[h, g] = tiles[slot, 0]
                else:
                    copy.start()

    for one in w_loads:
        one.wait()
    multiply(0, 1)
    for a in range(1, 4):
        for way, half in order:
            zcopy(way, a, half).wait_recv()
            if a < 3 or way == half:
                zcopy(way, a + 1, half).start()
        multiply(2 * a - 1, 2)
    zcopy(0, 4, 0).wait_recv()
    zcopy(1, 4, 1).wait_recv()
    multiply(7, 1)

    for dh in range(8):
        for i in range(4):
            if dh or i:
                hh, gg = lax.rem(h + dh, 8), lax.rem(g + i, 4)
                pltpu.make_async_remote_copy(
                    src_ref=tiles.at[0, 0], dst_ref=landed.at[hh, gg],
                    send_sem=rsend.at[0, 0], recv_sem=rrecv.at[hh, gg],
                    device_id=(z * 4 + gg, hh), device_id_type=MESH,
                ).wait_recv()
    total = landed[0].astype(F32)
    for n in range(1, 8):
        total = total + landed[n].astype(F32)
    out[...] = total.astype(BF16)

    for way, half in order:
        for a in range(1, 5):
            if a < 4 or way == half:
                zcopy(way, a, half).wait_send()
    for slot in range(8):
        to_head = slot_head(slot)
        for i in range(4):
            if i == 0:
                @pl.when(to_head != h)
                def _(slot=slot, to_head=to_head):
                    tile_copy(slot, 0, to_head).wait_send()
            else:
                tile_copy(slot, i, to_head).wait_send()


ANY = pl.BlockSpec(memory_space=pl.ANY)
VMEM = pl.BlockSpec(memory_space=pltpu.VMEM)
SMEM = pl.BlockSpec(memory_space=pltpu.SMEM)
DMA = pltpu.SemaphoreType.DMA


def attend(span_cache, destination, resident, block_table, lengths, new_latent, query, w_uk, w_uv, w_out):
    z, xl, c, y, xh = coords()
    owners = jnp.stack([peer_of(e, k, z, xl, c, y, 1) for e in range(2) for k in range(4)])
    named = destination[:, 0][None, :] == owners[:, None]
    at = lax.broadcasted_iota(jnp.int32, named.shape, 1)
    last = jnp.max(jnp.where(named, at, 0), axis=1)
    first = 31 - jnp.max(jnp.where(named, 31 - at, 0), axis=1)
    pick = jnp.stack([first, last, jnp.any(named, axis=1).astype(jnp.int32)], axis=1)

    rel, e, ab, k = (lax.broadcasted_iota(jnp.int32, (4, 2, 2, 4), d) for d in range(4))
    dz = lax.rem(y + rel + k, 4) + 4 * e
    source = lax.rem(z + 8 - dz, 8) * 4 + lax.rem(xl + k // 2, 2) * 2 + lax.rem(c + k, 2)
    pages = jnp.concatenate([jnp.arange(48, dtype=jnp.int32), (48 + source * 2 + ab).reshape(-1)])
    hit = block_table[:, :, None] == pages[None, None, :]
    col = jnp.arange(32, dtype=jnp.int32)[None, :, None]
    full = (lengths // 64)[:, None, None]
    count = jnp.sum((hit & (col < full)).astype(jnp.int32), axis=1)
    partial = jnp.sum((hit & (col == full)).astype(jnp.int32), axis=1)
    inside = jnp.arange(64, dtype=jnp.int32)[None, None, :] < lax.rem(lengths, 64)[:, None, None]
    reads = count[:, :, None] + partial[:, :, None] * inside.astype(jnp.int32)
    bias = jnp.log2(reads.astype(F32)).reshape(16, 112 * 64)

    q = query.transpose(2, 1, 0, 3).reshape(1024, 192)
    none = jnp.zeros((1024, 64), BF16)
    q3 = jnp.concatenate([q, none, none, q[:, 128:]], axis=1)

    return pl.pallas_call(
        attend_kernel,
        out_shape=(
            jax.ShapeDtypeStruct((64, 2048), BF16),
            jax.ShapeDtypeStruct((3, 2048, 224), BF16),
        ),
        in_specs=[SMEM, VMEM, VMEM, ANY, ANY, ANY, ANY, ANY, ANY],
        out_specs=(ANY, ANY),
        scratch_shapes=[
            pltpu.VMEM((32, 64, 576), BF16),
            pltpu.VMEM((3072, 576), BF16),
            pltpu.VMEM((16, 128, 512), BF16),
            pltpu.VMEM((16, 512, 128), BF16),
            pltpu.VMEM((64, 576), BF16),
            pltpu.VMEM((8, 9, 64, 128), BF16),
            pltpu.VMEM((4, 2, 9, 4, 64, 128), BF16),
            pltpu.VMEM((1024, 512), BF16),
            pltpu.VMEM((1024, 512), F32),
            pltpu.VMEM((1024, 128), F32),
            pltpu.VMEM((1024, 128), F32),
            pltpu.VMEM((64, 2048), BF16),
            DMA((4,)), DMA((6,)), DMA((8,)), DMA((8,)),
            DMA((2, 2, 8)), DMA((2, 2, 8)), DMA((3,)), DMA((3,)), DMA,
        ],
        compiler_params=pltpu.CompilerParams(
            collective_id=0, has_side_effects=True, vmem_limit_bytes=56 * 1024 * 1024
        ),
        name="handoff_attend",
    )(pick, q3, bias, span_cache, resident.reshape(3072, 576), new_latent.reshape(64, 576), w_uk, w_uv, w_out)


def project(heads, w_out, wall):
    out = pl.pallas_call(
        project_kernel,
        out_shape=jax.ShapeDtypeStruct((4, 64, 224), BF16),
        in_specs=[ANY, ANY, ANY],
        out_specs=VMEM,
        scratch_shapes=[
            pltpu.VMEM((4, 2048, 224), BF16),
            pltpu.VMEM((8, 64, 2048), BF16),
            pltpu.VMEM((8, 4, 64, 224), BF16),
            pltpu.VMEM((8, 4, 64, 224), BF16),
            DMA((5,)), DMA((2, 4, 2)), DMA((2, 4, 2)), DMA((8, 4)), DMA((8, 4)),
        ],
        compiler_params=pltpu.CompilerParams(
            collective_id=1, has_side_effects=True, vmem_limit_bytes=56 * 1024 * 1024
        ),
        name="gather_project",
    )(heads, w_out, wall)
    return out.reshape(4, 4, 16, 224).transpose(0, 2, 1, 3).reshape(64, 4, 224)


def per_device(
    span_cache, destination, resident, block_table, lengths, new_latent, query, w_uk, w_uv, w_out
):
    heads, wall = attend(
        span_cache, destination, resident, block_table, lengths, new_latent, query, w_uk, w_uv, w_out
    )
    return project(heads, w_out, wall)


def solution(mesh):
    return jax.shard_map(
        per_device,
        mesh=mesh,
        in_specs=(
            P("pool", None, None),
            P("pool", None),
            P("pool", None, None),
            P("pool", None),
            P("pool"),
            P("pool", None, None),
            P("pool", None, "head", None),
            P("head", None, None),
            P("head", None, None),
            P("head", "pool"),
        ),
        out_specs=P("head", None, "pool"),
        check_vma=False,
    )
```

```python
import functools

import jax
import jax.numpy as jnp
from jax import lax
from jax.experimental import pallas as pl
from jax.experimental.pallas import tpu as pltpu
from jax.sharding import PartitionSpec as P

MESH = pl.DeviceIdType.MESH
F32 = jnp.float32
BF16 = jnp.bfloat16
NT = (((1,), (1,)), ((), ()))
QT = 1024
SENT = (8, 9, 10, 0, 1, 2, 3, 4, 5, 6, 7)


def coords():
    p = lax.axis_index("pool")
    h = lax.axis_index("head")
    return p // 4, lax.rem(p // 2, 2), lax.rem(p, 2), h // 2, lax.rem(h, 2)


DIRECT = ((0, 0), (0, 1), (0, 2), (0, 3), (1, 0), (1, 1), (7, 0), (7, 1))


def split_offset(i, y, xh):
    dz0 = jnp.where(i == 0, 1 + 6 * (y // 2), jnp.where(i == 1, 3, 5))
    k0 = jnp.where(i == 0, 2 + lax.rem(y, 2), lax.rem(y + i, 4))
    dz1 = jnp.where(i == 0, 2, jnp.where(i == 1, 6, 4))
    k1 = lax.rem(y + i, 4)
    return jnp.where(xh == 0, dz0, dz1), jnp.where(xh == 0, k0, k1)


def offset_of(j, y, xh):
    return DIRECT[j] if j < 8 else split_offset(j - 8, y, xh)


def peer_of(j, z, xl, c, y, xh, sign):
    dz, k = offset_of(j, y, xh)
    return lax.rem(z + 8 + sign * dz, 8) * 4 + lax.rem(xl + k // 2, 2) * 2 + lax.rem(c + k, 2)


def attend_kernel(
    pick, q3, bias, span, resident, fresh, w_uk, w_uv, w_out,
    heads_out, wall,
    span_v, res_v, uk_v, uv_v, fresh_v, bias_v, sendbuf, near, arr, q_main, q_low, q_high, turned, acc, m_s, l_s, out_v,
    load_sem, res_sem, zsend, zrecv, xsend, xrecv, ysend, yrecv, wsend, wrecv, out_sem,
):
    z, xl, c, y, xh = coords()
    p = lax.axis_index("pool")
    h = lax.axis_index("head")
    g = lax.rem(p, 4)
    up = lax.rem(y + 1, 4) * 2 + xh
    down = lax.rem(y + 3, 4) * 2 + xh
    across = y * 2 + 1 - xh
    core_mate = p + 1 - 2 * c
    xl_mate = p + 2 - 4 * xl

    loads = [
        pltpu.make_async_copy(span, span_v, load_sem.at[0]),
        pltpu.make_async_copy(w_uk, uk_v, load_sem.at[1]),
        pltpu.make_async_copy(fresh, fresh_v, load_sem.at[2]),
        pltpu.make_async_copy(w_uv, uv_v, load_sem.at[3]),
    ]
    res_loads = [
        pltpu.make_async_copy(resident.at[pl.ds(512 * n, 512)], res_v.at[pl.ds(512 * n, 512)], res_sem.at[n])
        for n in range(6)
    ]
    bias_load = pltpu.make_async_copy(bias, bias_v, load_sem.at[4])
    loads[0].start()

    barrier = pltpu.get_barrier_semaphore()

    def greet(pool_to, head_to):
        pl.semaphore_signal(barrier, inc=1, device_id=(pool_to, head_to), device_id_type=MESH)

    for j in range(1, 11):
        for sign in (1, -1):
            greet(peer_of(j, z, xl, c, y, xh, sign), h)
    greet(p, up)
    greet(p, down)
    greet(core_mate, h)
    greet(xl_mate, h)
    greet(p, across)

    loads[0].wait()
    for one in loads[1:3] + res_loads[:2] + [bias_load] + res_loads[2:] + loads[3:]:
        one.start()
    zcopies = {}
    for j in SENT:
        live = pick[0, j] >= 0
        for ab in range(2):
            at = jnp.maximum(pick[0, j], 0) if ab else 31 - jnp.maximum(pick[1, j], 0)
            block = span_v[at] * live.astype(F32).astype(BF16)
            for slab in range(4):
                sendbuf[j, ab * 4 + slab] = block[:, slab * 128 : (slab + 1) * 128]
            if ab == 0:
                low = block[:, 512:]
            else:
                sendbuf[j, 8] = jnp.concatenate([low, block[:, 512:]], axis=1)
        landing = near.at[j // 4, :, j % 4] if j < 8 else arr.at[0, :, j - 8]
        if j == 0:
            keep = pltpu.make_async_copy(sendbuf.at[0], landing, zrecv.at[0])
            keep.start()
            continue
        zcopies[j] = pltpu.make_async_remote_copy(
            src_ref=sendbuf.at[j], dst_ref=landing, send_sem=zsend.at[j], recv_sem=zrecv.at[j],
            device_id=(peer_of(j, z, xl, c, y, xh, 1), h), device_id_type=MESH,
        )
        if j == 10:
            pl.semaphore_wait(barrier, 25)
            for one in (8, 9, 10):
                zcopies[one].start()
        if j in (1, 2, 3):
            zcopies[j].start()

    def wcopy(src, owner, to, n):
        slot = lax.rem(owner - lax.rem(to, 4) + 4, 4) - 1
        return pltpu.make_async_remote_copy(
            src_ref=src, dst_ref=wall.at[slot], send_sem=wsend.at[n], recv_sem=wrecv.at[n],
            device_id=(to, h), device_id_type=MESH,
        )

    w_mate = wcopy(w_out, g, core_mate, 0)
    w_far = wcopy(w_out, g, xl_mate, 1)
    w_pass = wcopy(wall.at[1], lax.rem(g + 2, 4), core_mate, 2)
    loads[1].wait()

    @pl.loop(0, 8)
    def _(two):
        cols = pl.ds(pl.multiple_of(two * 128, 128), 128)
        both = []
        for n in range(2):
            at = pl.ds(pl.multiple_of(two * 128 + n * 64, 64), 64)
            both.append(jnp.dot(q3[at, :128], uk_v[two * 2 + n], preferred_element_type=F32))
        q_main[:, cols] = jnp.concatenate(both, axis=0).astype(BF16).T
        rope = q3[cols, 128:192].T
        none = jnp.zeros((64, 128), BF16)
        q_low[:, cols] = jnp.concatenate([rope, none], axis=0)
        q_high[:, cols] = jnp.concatenate([none, rope], axis=0)

    scale = 1.4426950408889634 * 192 ** -0.5

    def fold(cols, s, values, first=False):
        top = jnp.max(s, axis=0, keepdims=True)
        if not first:
            before = m_s[:1, cols]
            top = jnp.maximum(top, before)
        p_ = jnp.exp2(s - top)
        total = jnp.sum(p_, axis=0, keepdims=True)
        mix = jnp.dot(values, p_.astype(BF16), preferred_element_type=F32)
        if not first:
            fade = jnp.exp2(before - top)
            total = total + l_s[:1, cols] * fade
            mix = mix + acc[:, cols] * fade
        acc[:, cols] = mix
        m_s[:1, cols] = top
        l_s[:1, cols] = total

    def each_tile(body):
        for t in range(1024 // QT):
            body(pl.ds(t * QT, QT))

    loads[2].wait()
    new = fresh_v[...].reshape(64, 576)
    turned[:, :64] = new[:, :512].T

    def fresh_tile(cols):
        s = jnp.dot(new[:, :512], q_main[:, cols], preferred_element_type=F32)
        s = s + jnp.dot(new[:, 512:], q_low[:64, cols], preferred_element_type=F32)
        token = lax.broadcasted_iota(jnp.int32, s.shape, 0)
        lane = lax.broadcasted_iota(jnp.int32, s.shape, 1)
        seen = ((lane & 15) == (token >> 2)) & (((lane >> 4) & 3) >= (token & 3))
        fold(cols, jnp.where(seen, s * scale, -jnp.inf), turned[:, :64], first=True)

    each_tile(fresh_tile)

    def biased(s, toks):
        b = bias_v[toks, :]
        return s * scale + jnp.concatenate([b] * (QT // 128), axis=1)

    def resident_chunk(n):
        res_loads[n].wait()
        toks = pl.ds(512 * n, 512)
        turned[:, :512] = res_v[toks, :512].T

        def tile(cols):
            s = jnp.dot(res_v[toks, :512], q_main[:, cols], preferred_element_type=F32)
            s = s + jnp.dot(res_v[toks, 512:], q_low[:64, cols], preferred_element_type=F32)
            fold(cols, biased(s, toks), turned[:, :512])

        each_tile(tile)

    def arrived_chunk(held, first, count):
        half = 64 * count
        for ab in range(2):
            for j in range(4):
                turned[j * 128 : (j + 1) * 128, ab * half : (ab + 1) * half] = (
                    held[ab * 4 + j].reshape(half, 128).T
                )

        def tile(cols):
            rope = held[8].reshape(half, 128)
            main = jnp.concatenate(
                [
                    jnp.concatenate([held[ab * 4 + j].reshape(half, 128) for j in range(4)], axis=1)
                    for ab in range(2)
                ],
                axis=0,
            )
            s = jnp.dot(main, q_main[:, cols], preferred_element_type=F32)
            s = s + jnp.concatenate(
                [jnp.dot(rope, q[:, cols], preferred_element_type=F32) for q in (q_low, q_high)], axis=0
            )
            fold(cols, biased(s, pl.ds(first, 2 * half)), turned[:, : 2 * half])

        each_tile(tile)

    def near_chunk(n):
        arrived_chunk(near.at[n], 3072 + 512 * n, 4)

    def far_chunk(rel):
        arrived_chunk(arr.at[rel], 4096 + 768 * rel, 6)

    def ycopy(i, way, kind):
        landing = 2 if kind else (3 if way == 0 else 1)
        source = 0 if kind == 0 else (3 if way == 0 else 1)
        return pltpu.make_async_remote_copy(
            src_ref=arr.at[source, :, i], dst_ref=arr.at[landing, :, i],
            send_sem=ysend.at[way, kind, i], recv_sem=yrecv.at[way, kind, i],
            device_id=(p, up if way == 0 else down), device_id_type=MESH,
        )

    def xcopy(i):
        return pltpu.make_async_remote_copy(
            src_ref=arr.at[0, :, i], dst_ref=arr.at[0, :, 3 + i],
            send_sem=xsend.at[i], recv_sem=xrecv.at[i], device_id=(p, across), device_id_type=MESH,
        )

    def own_step(i):
        if i < 3:
            zcopies[8 + i].wait_recv()
            xcopy(i).start()
        else:
            xcopy(i - 3).wait_recv()
        ycopy(i, 0, 0).start()
        ycopy(i, 1, 0).start()

    def pass_step(i):
        ycopy(i, 0, 0).wait_recv()
        ycopy(i, 1, 0).wait_recv()
        ycopy(i, i % 2, 1).start()

    bias_load.wait()
    resident_chunk(0)
    own_step(0)
    resident_chunk(1)
    resident_chunk(2)
    own_step(1)
    own_step(2)
    for j in (8, 9, 10):
        zcopies[j].wait_send()
    for j in (4, 5, 6, 7):
        zcopies[j].start()
    own_step(3)
    pass_step(0)
    resident_chunk(3)
    own_step(4)
    own_step(5)
    w_mate.start()
    w_far.start()
    resident_chunk(4)
    pass_step(1)
    pass_step(2)
    resident_chunk(5)
    keep.wait()
    for j in (1, 2, 3):
        zcopies[j].wait_recv()
    pass_step(3)
    near_chunk(0)
    pass_step(4)
    pass_step(5)
    far_chunk(0)
    far_chunk(3)
    far_chunk(1)
    for j in (4, 5, 6, 7):
        zcopies[j].wait_recv()
    near_chunk(1)
    w_far.wait_recv()
    w_pass.start()
    for i in range(6):
        ycopy(i, i % 2, 1).wait_recv()
    far_chunk(2)

    loads[3].wait()

    @pl.loop(0, 8)
    def _(two):
        cols = pl.ds(pl.multiple_of(two * 128, 128), 128)
        mixed = (acc[:, cols] / l_s[:1, cols]).astype(BF16).T
        for n in range(2):
            out_v[:, pl.ds(pl.multiple_of(two * 256 + n * 128, 128), 128)] = jnp.dot(
                mixed[n * 64 : (n + 1) * 64], uv_v[two * 2 + n], preferred_element_type=F32
            ).astype(BF16)

    done = pltpu.make_async_copy(out_v, heads_out, out_sem)
    done.start()

    for j in range(1, 8):
        zcopies[j].wait_send()
    for i in range(3):
        xcopy(i).wait_send()
    for i in range(6):
        ycopy(i, 0, 0).wait_send()
        ycopy(i, 1, 0).wait_send()
        ycopy(i, i % 2, 1).wait_send()
    w_mate.wait()
    w_far.wait_send()
    w_pass.wait()
    done.wait()


def project_kernel(
    heads, w_out, wall,
    out,
    w_v, hbuf, tiles, landed, load_sem, zsend, zrecv, rsend, rrecv,
):
    p = lax.axis_index("pool")
    h = lax.axis_index("head")
    z, g = p // 4, lax.rem(p, 4)
    right = lax.rem(z + 1, 8) * 4 + g
    left = lax.rem(z + 7, 8) * 4 + g

    own = pltpu.make_async_copy(heads, hbuf.at[0], load_sem.at[4])
    own.start()
    w_loads = [pltpu.make_async_copy(w_out, w_v.at[0], load_sem.at[0])] + [
        pltpu.make_async_copy(wall.at[i], w_v.at[i + 1], load_sem.at[i + 1]) for i in range(3)
    ]
    for one in w_loads:
        one.start()

    barrier = pltpu.get_barrier_semaphore()

    def greet(pool_to, head_to):
        pl.semaphore_signal(barrier, inc=1, device_id=(pool_to, head_to), device_id_type=MESH)

    greet(right, h)
    greet(left, h)
    for dh in range(8):
        for i in range(4):
            if dh or i:
                greet(z * 4 + lax.rem(g + i, 4), lax.rem(h + dh, 8))
    pl.semaphore_wait(barrier, 33)

    def zcopy(way, a, half):
        rows = pl.ds(32 * half, 32)
        src = 0 if a == 1 else 2 * (a - 1) - 1 + way
        dst = 7 if a == 4 else 2 * a - 1 + way
        return pltpu.make_async_remote_copy(
            src_ref=hbuf.at[src, rows], dst_ref=hbuf.at[dst, rows],
            send_sem=zsend.at[way, a - 1, half], recv_sem=zrecv.at[way, a - 1, half],
            device_id=(right if way == 0 else left, h), device_id_type=MESH,
        )

    own.wait()
    order = [(0, 0), (0, 1), (1, 1), (1, 0)]
    for way, half in order:
        zcopy(way, 1, half).start()

    def tile_copy(slot, i, to_head):
        return pltpu.make_async_remote_copy(
            src_ref=tiles.at[slot, i], dst_ref=landed.at[h, g],
            send_sem=rsend.at[slot, i], recv_sem=rrecv.at[h, g],
            device_id=(z * 4 + lax.rem(g + i, 4), to_head), device_id_type=MESH,
        )

    def slot_head(slot):
        if slot == 0:
            return z
        if slot == 7:
            return lax.rem(z + 4, 8)
        a = (slot + 1) // 2
        return lax.rem(z + 8 - a, 8) if slot % 2 else lax.rem(z + a, 8)

    def multiply(first, count):
        lhs = hbuf[pl.ds(first, count)].reshape(64 * count, 2048)
        for i in range(4):
            part = lax.dot_general(lhs, w_v[i], NT, preferred_element_type=F32).astype(BF16)
            for n in range(count):
                slot = first + n
                to_head = slot_head(slot)
                tiles[slot, i] = part[64 * n : 64 * (n + 1)]
                copy = tile_copy(slot, i, to_head)
                if i == 0:
                    @pl.when(to_head != h)
                    def _(copy=copy):
                        copy.start()

                    @pl.when(to_head == h)
                    def _(slot=slot):
                        landed[h, g] = tiles[slot, 0]
                else:
                    copy.start()

    for one in w_loads:
        one.wait()
    multiply(0, 1)
    for a in range(1, 4):
        for way, half in order:
            zcopy(way, a, half).wait_recv()
            if a < 3 or way == half:
                zcopy(way, a + 1, half).start()
        multiply(2 * a - 1, 2)
    zcopy(0, 4, 0).wait_recv()
    zcopy(1, 4, 1).wait_recv()
    multiply(7, 1)

    for dh in range(8):
        for i in range(4):
            if dh or i:
                hh, gg = lax.rem(h + dh, 8), lax.rem(g + i, 4)
                pltpu.make_async_remote_copy(
                    src_ref=tiles.at[0, 0], dst_ref=landed.at[hh, gg],
                    send_sem=rsend.at[0, 0], recv_sem=rrecv.at[hh, gg],
                    device_id=(z * 4 + gg, hh), device_id_type=MESH,
                ).wait_recv()
    total = landed[0].astype(F32)
    for n in range(1, 8):
        total = total + landed[n].astype(F32)
    out[...] = total.astype(BF16)

    for way, half in order:
        for a in range(1, 5):
            if a < 4 or way == half:
                zcopy(way, a, half).wait_send()
    for slot in range(8):
        to_head = slot_head(slot)
        for i in range(4):
            if i == 0:
                @pl.when(to_head != h)
                def _(slot=slot, to_head=to_head):
                    tile_copy(slot, 0, to_head).wait_send()
            else:
                tile_copy(slot, i, to_head).wait_send()


ANY = pl.BlockSpec(memory_space=pl.ANY)
VMEM = pl.BlockSpec(memory_space=pltpu.VMEM)
SMEM = pl.BlockSpec(memory_space=pltpu.SMEM)
DMA = pltpu.SemaphoreType.DMA


def attend(span_cache, destination, resident, block_table, lengths, new_latent, query, w_uk, w_uv, w_out):
    z, xl, c, y, xh = coords()
    near = jnp.array(DIRECT, jnp.int32)
    dz, k = split_offset(jnp.arange(3, dtype=jnp.int32), y, xh)
    dz, k = jnp.concatenate([near[:, 0], dz]), jnp.concatenate([near[:, 1], k])
    owners = lax.rem(z + dz, 8) * 4 + lax.rem(xl + k // 2, 2) * 2 + lax.rem(c + k, 2)
    at = jnp.arange(32, dtype=jnp.int32)
    places = jnp.stack([at, 31 - at])[:, None, :]
    pick = jnp.max(jnp.where(destination[:, 0] == owners[:, None], places, -1), axis=2)

    member = lax.rem(y + jnp.arange(4, dtype=jnp.int32)[:, None], 4)
    m = jnp.arange(6, dtype=jnp.int32)[None, :]
    far_dz, far_k = split_offset(lax.rem(m, 3), member, lax.rem(xh + m // 3, 2))

    def slots(dz, k):
        source = lax.rem(z + 8 - dz, 8) * 4 + lax.rem(xl + k // 2, 2) * 2 + lax.rem(c + k, 2)
        return (48 + 2 * source[:, None, :] + jnp.arange(2, dtype=jnp.int32)[None, :, None]).reshape(-1)

    pages = jnp.concatenate([
        jnp.arange(48, dtype=jnp.int32),
        slots(near[:, 0].reshape(2, 4), near[:, 1].reshape(2, 4)),
        slots(far_dz, far_k),
    ])
    table = jnp.tile(block_table.T, (1, 8))
    length = jnp.tile(lengths, 8)
    hit = table[None, :, :] == pages[:, None, None]
    col = jnp.arange(32, dtype=jnp.int32)[None, :, None]
    full = (length // 64)[None, None, :]
    count = jnp.sum((hit & (col < full)).astype(F32), axis=1)
    partial = jnp.sum((hit & (col == full)).astype(F32), axis=1)
    inside = jnp.arange(64, dtype=jnp.int32)[:, None] < lax.rem(length, 64)[None, :]
    reads = count[:, None, :] + jnp.where(inside[None], partial[:, None, :], 0.0)
    bias = jnp.log2(reads).reshape(112 * 64, 128)

    q3 = query.transpose(2, 1, 0, 3).reshape(1024, 192)

    return pl.pallas_call(
        attend_kernel,
        out_shape=(
            jax.ShapeDtypeStruct((64, 2048), BF16),
            jax.ShapeDtypeStruct((3, 224, 2048), BF16),
        ),
        in_specs=[SMEM, VMEM, ANY, ANY, ANY, ANY, ANY, ANY, ANY],
        out_specs=(ANY, ANY),
        scratch_shapes=[
            pltpu.VMEM((32, 64, 576), BF16),
            pltpu.VMEM((3072, 576), BF16),
            pltpu.VMEM((16, 128, 512), BF16),
            pltpu.VMEM((16, 512, 128), BF16),
            pltpu.VMEM((16, 4, 576), BF16),
            pltpu.VMEM((7168, 128), F32),
            pltpu.VMEM((11, 9, 64, 128), BF16),
            pltpu.VMEM((2, 9, 4, 64, 128), BF16),
            pltpu.VMEM((4, 9, 6, 64, 128), BF16),
            pltpu.VMEM((512, 1024), BF16),
            pltpu.VMEM((128, 1024), BF16),
            pltpu.VMEM((128, 1024), BF16),
            pltpu.VMEM((512, 768), BF16),
            pltpu.VMEM((512, 1024), F32),
            pltpu.VMEM((8, 1024), F32),
            pltpu.VMEM((8, 1024), F32),
            pltpu.VMEM((64, 2048), BF16),
            DMA((5,)), DMA((6,)), DMA((11,)), DMA((11,)), DMA((3,)), DMA((3,)),
            DMA((2, 2, 6)), DMA((2, 2, 6)), DMA((3,)), DMA((3,)), DMA,
        ],
        compiler_params=pltpu.CompilerParams(
            collective_id=0, has_side_effects=True, vmem_limit_bytes=56 * 1024 * 1024
        ),
        name="handoff_attend",
    )(pick, q3, bias, span_cache, resident.reshape(3072, 576), new_latent, w_uk, w_uv, w_out)


def project(heads, w_out, wall):
    out = pl.pallas_call(
        project_kernel,
        out_shape=jax.ShapeDtypeStruct((4, 64, 224), BF16),
        in_specs=[ANY, ANY, ANY],
        out_specs=VMEM,
        scratch_shapes=[
            pltpu.VMEM((4, 224, 2048), BF16),
            pltpu.VMEM((8, 64, 2048), BF16),
            pltpu.VMEM((8, 4, 64, 224), BF16),
            pltpu.VMEM((8, 4, 64, 224), BF16),
            DMA((5,)), DMA((2, 4, 2)), DMA((2, 4, 2)), DMA((8, 4)), DMA((8, 4)),
        ],
        compiler_params=pltpu.CompilerParams(
            collective_id=1, has_side_effects=True, vmem_limit_bytes=56 * 1024 * 1024
        ),
        name="gather_project",
    )(heads, w_out, wall)
    return out.reshape(4, 4, 16, 224).transpose(0, 2, 1, 3).reshape(64, 4, 224)


def per_device(
    span_cache, destination, resident, block_table, lengths, new_latent, query, w_uk, w_uv, w_out
):
    w_out = w_out.T
    heads, wall = attend(
        span_cache, destination, resident, block_table, lengths, new_latent, query, w_uk, w_uv, w_out
    )
    return project(heads, w_out, wall)


def solution(mesh):
    return jax.shard_map(
        per_device,
        mesh=mesh,
        in_specs=(
            P("pool", None, None),
            P("pool", None),
            P("pool", None, None),
            P("pool", None),
            P("pool"),
            P("pool", None, None),
            P("pool", None, "head", None),
            P("head", None, None),
            P("head", None, None),
            P("head", "pool"),
        ),
        out_specs=P("head", None, "pool"),
        check_vma=False,
    )
```

```python
import functools

import jax
import jax.numpy as jnp
from jax import lax
from jax.experimental import pallas as pl
from jax.experimental.pallas import tpu as pltpu
from jax.sharding import PartitionSpec as P

MESH = pl.DeviceIdType.MESH
F32 = jnp.float32
BF16 = jnp.bfloat16
NT = (((1,), (1,)), ((), ()))
QT = 1024
SENT = (8, 9, 10, 0, 1, 2, 3, 4, 5, 6, 7)


def coords():
    p = lax.axis_index("pool")
    h = lax.axis_index("head")
    return p // 4, lax.rem(p // 2, 2), lax.rem(p, 2), h // 2, lax.rem(h, 2)


DIRECT = ((0, 0), (0, 1), (0, 2), (0, 3), (1, 0), (1, 1), (7, 0), (7, 1))


def split_offset(i, y, xh):
    dz0, k0 = (1 + 6 * (y // 2), 2 + lax.rem(y, 2)) if i == 0 else (2 * i + 1, lax.rem(y + i, 4))
    dz1, k1 = (2, 6, 4)[i], lax.rem(y + i, 4)
    return jnp.where(xh == 0, dz0, dz1), jnp.where(xh == 0, k0, k1)


def offset_of(j, y, xh):
    return DIRECT[j] if j < 8 else split_offset(j - 8, y, xh)


def peer_of(j, z, xl, c, y, xh, sign):
    dz, k = offset_of(j, y, xh)
    return pool_at(dz, k, z, xl, c, sign)


def pool_at(dz, k, z, xl, c, sign):
    return lax.rem(z + 8 + sign * dz, 8) * 4 + lax.rem(xl + k // 2, 2) * 2 + lax.rem(c + k, 2)


def kernel(
    dest, table, query, span, resident, fresh, w_uk, w_uv, w_out,
    out,
    span_v, res_v, uk_v, uv_v, fresh_v, query_v, query_f, bias_v, sendbuf, near, arr, q_main, q_low, q_high, turned,
    acc, m_s, l_s, w_v, hbuf, tiles, landed,
    load_sem, res_sem, zsend, zrecv, xsend, xrecv, ysend, yrecv, wsend, wrecv, hsend, hrecv, rsend, rrecv,
):
    z, xl, c, y, xh = coords()
    p = lax.axis_index("pool")
    h = lax.axis_index("head")
    g = lax.rem(p, 4)
    up = lax.rem(y + 1, 4) * 2 + xh
    down = lax.rem(y + 3, 4) * 2 + xh
    across = y * 2 + 1 - xh
    core_mate = p + 1 - 2 * c
    xl_mate = p + 2 - 4 * xl
    right = lax.rem(z + 1, 8) * 4 + g
    left = lax.rem(z + 7, 8) * 4 + g

    load = lambda src, dst, n: pltpu.make_async_copy(src, dst, load_sem.at[n])
    span_load = load(span, span_v, 0)
    query_load = load(query, query_v, 1)
    uk_load = load(w_uk, uk_v, 2)
    fresh_load = load(fresh, fresh_v, 3)
    uv_load = load(w_uv, uv_v, 4)
    w_load = load(w_out, w_v.at[0], 5)
    res_loads = [
        pltpu.make_async_copy(resident.at[pl.ds(512 * n, 512)], res_v.at[pl.ds(512 * n, 512)], res_sem.at[n])
        for n in range(6)
    ]
    span_load.start()

    barrier = pltpu.get_barrier_semaphore()

    def greet(pool_to, head_to):
        pl.semaphore_signal(barrier, inc=1, device_id=(pool_to, head_to), device_id_type=MESH)

    for j in range(1, 11):
        for sign in (1, -1):
            greet(peer_of(j, z, xl, c, y, xh, sign), h)
    greet(p, up)
    greet(p, down)
    greet(p, across)
    greet(core_mate, h)
    greet(xl_mate, h)
    greet(right, h)
    greet(left, h)
    for dh in range(8):
        for i in range(4):
            if dh or i:
                greet(z * 4 + lax.rem(g + i, 4), lax.rem(h + dh, 8))

    owners = [peer_of(j, z, xl, c, y, xh, 1) for j in range(11)]
    last = [jnp.int32(-1)] * 11
    first = [jnp.int32(-1)] * 11
    for b in range(32):
        ahead, behind = dest[b, 0], dest[31 - b, 0]
        for j in range(11):
            last[j] = jnp.where(ahead == owners[j], b, last[j])
            first[j] = jnp.where(behind == owners[j], 31 - b, first[j])

    span_load.wait()
    for one in [query_load, uk_load, fresh_load] + res_loads + [uv_load, w_load]:
        one.start()
    zcopies = {}
    for j in SENT:
        live = (last[j] >= 0).astype(F32).astype(BF16)
        for ab in range(2):
            block = span_v[jnp.maximum(last[j] if ab else first[j], 0)] * live
            for slab in range(4):
                sendbuf[j, ab * 4 + slab] = block[:, slab * 128 : (slab + 1) * 128]
            if ab == 0:
                low = block[:, 512:]
            else:
                sendbuf[j, 8] = jnp.concatenate([low, block[:, 512:]], axis=1)
        if j == 0:
            keep = pltpu.make_async_copy(sendbuf.at[0], near.at[0, :, 0], zrecv.at[0])
            keep.start()
            continue
        zcopies[j] = pltpu.make_async_remote_copy(
            src_ref=sendbuf.at[j],
            dst_ref=near.at[j // 4, :, j % 4] if j < 8 else arr.at[0, :, j - 8],
            send_sem=zsend.at[j],
            recv_sem=zrecv.at[j],
            device_id=(peer_of(j, z, xl, c, y, xh, 1), h), device_id_type=MESH,
        )
        if j == 8:
            pl.semaphore_wait(barrier, 58)
        if j in (8, 9, 10, 1, 2, 3):
            zcopies[j].start()

    def wcopy(src, owner, to, n):
        slot = lax.rem(owner - lax.rem(to, 4) + 4, 4)
        return pltpu.make_async_remote_copy(
            src_ref=src, dst_ref=w_v.at[slot], send_sem=wsend.at[n], recv_sem=wrecv.at[n],
            device_id=(to, h), device_id_type=MESH,
        )

    w_mate = wcopy(w_out, g, core_mate, 0)
    w_far = wcopy(w_out, g, xl_mate, 1)
    w_pass = wcopy(w_v.at[2], lax.rem(g + 2, 4), core_mate, 2)

    query_load.wait()
    query_f[0] = query_v[:, :128].astype(F32)
    query_f[1] = jnp.concatenate([query_v[:, 128:].astype(F32), jnp.zeros((1024, 64), F32)], axis=1)
    uk_load.wait()

    @pl.loop(0, 8)
    def _(two):
        cols = pl.ds(pl.multiple_of(two * 128, 128), 128)
        plain, rope = (
            jnp.concatenate([query_f[part, pl.ds(two * 2 + n, 64, stride=16), :] for n in range(2)], axis=0).astype(BF16)
            for part in range(2)
        )
        q_main[:, cols] = jnp.concatenate(
            [
                jnp.dot(plain[64 * n : 64 * (n + 1)], uk_v[two * 2 + n], preferred_element_type=F32)
                for n in range(2)
            ],
            axis=0,
        ).astype(BF16).T
        rope = rope.T
        q_low[:, cols] = rope
        q_high[:, cols] = jnp.concatenate([rope[64:], rope[:64]], axis=0)

    scale = 1.4426950408889634 * 192 ** -0.5

    def fold(cols, s, values, first=False):
        top = jnp.max(s, axis=0, keepdims=True)
        if not first:
            before = m_s[:1, cols]
            top = jnp.maximum(top, before)
        p_ = jnp.exp2(s - top)
        total = jnp.sum(p_, axis=0, keepdims=True)
        mix = jnp.dot(values, p_.astype(BF16), preferred_element_type=F32)
        if not first:
            fade = jnp.exp2(before - top)
            total = total + l_s[:1, cols] * fade
            mix = mix + acc[:, cols] * fade
        acc[:, cols] = mix
        m_s[:1, cols] = top
        l_s[:1, cols] = total

    fresh_load.wait()
    new = fresh_v[...].reshape(64, 576)
    turned[:, :64] = new[:, :512].T
    ALL = pl.ds(0, 1024)
    s = jnp.dot(new[:, :512], q_main[...], preferred_element_type=F32)
    s = s + jnp.dot(new[:, 512:], q_low[:64, :], preferred_element_type=F32)
    token = lax.broadcasted_iota(jnp.int32, s.shape, 0)
    lane = lax.broadcasted_iota(jnp.int32, s.shape, 1)
    seen = (((lane >> 2) & 15) == (token >> 2)) & ((lane & 3) >= (token & 3))
    fold(ALL, jnp.where(seen, s * scale, -jnp.inf), turned[:, :64], first=True)

    length = table[32:33, :]
    whole = length >> 6
    position = lax.broadcasted_iota(jnp.int32, (32, 128), 0)
    full = jnp.where(position < whole, table[:32, :], -1)
    partial = jnp.max(jnp.where(position == whole, table[:32, :], -1), axis=0, keepdims=True)
    inside = lax.broadcasted_iota(jnp.int32, (64, 128), 0) < (length & 63)

    def fill_bias(n, page):
        count = jnp.sum(jnp.where(full == page, 1.0, 0.0), axis=0, keepdims=True)
        reads = count + jnp.where(inside & (partial == page), 1.0, 0.0)
        bias_v[64 * n : 64 * (n + 1), :] = jnp.where(reads > 0, jnp.log2(jnp.maximum(reads, 1.0)), -jnp.inf)

    def fill_pairs(n, offsets):
        for ab in range(2):
            for m, (dz, k) in enumerate(offsets):
                fill_bias(n + ab * len(offsets) + m, 48 + 2 * pool_at(dz, k, z, xl, c, -1) + ab)

    def biased(s, toks, width):
        b = bias_v[toks, :]
        return s * scale + jnp.concatenate([b] * (width // 128), axis=1)

    def resident_chunk(n):
        for page in range(8 * n, 8 * n + 8):
            fill_bias(page, page)
        res_loads[n].wait()
        toks = pl.ds(512 * n, 512)
        turned[:, :512] = res_v[toks, :512].T
        s = jnp.dot(res_v[toks, :512], q_main[...], preferred_element_type=F32)
        s = s + jnp.dot(res_v[toks, 512:], q_low[:64, :], preferred_element_type=F32)
        fold(ALL, biased(s, toks, 1024), turned[:, :512])

    def arrived_chunk(held, first, count, tiles_of=(ALL,), after=None):
        half = 64 * count
        for ab in range(2):
            for j in range(4):
                turned[j * 128 : (j + 1) * 128, ab * half : (ab + 1) * half] = (
                    held[ab * 4 + j].reshape(half, 128).T
                )
        for cols in tiles_of:
            rope = held[8].reshape(half, 128)
            main = jnp.concatenate(
                [
                    jnp.concatenate([held[ab * 4 + j].reshape(half, 128) for j in range(4)], axis=1)
                    for ab in range(2)
                ],
                axis=0,
            )
            s = jnp.dot(main, q_main[:, cols], preferred_element_type=F32)
            s = s + jnp.concatenate(
                [jnp.dot(rope, q[:, cols], preferred_element_type=F32) for q in (q_low, q_high)], axis=0
            )
            fold(cols, biased(s, pl.ds(first, 2 * half), cols.size), turned[:, : 2 * half])
            if after is not None:
                after(cols)

    def near_chunk(n):
        fill_pairs(48 + 8 * n, DIRECT[4 * n : 4 * n + 4])
        arrived_chunk(near.at[n], 3072 + 512 * n, 4)

    def far_bias(rel):
        member = lax.rem(y + rel, 4)
        fill_pairs(64 + 12 * rel, [split_offset(m % 3, member, lax.rem(xh + m // 3, 2)) for m in range(6)])

    def far_chunk(rel, **how):
        arrived_chunk(arr.at[rel], 4096 + 768 * rel, 6, **how)

    def xcopy(i):
        return pltpu.make_async_remote_copy(
            src_ref=arr.at[0, :, i], dst_ref=arr.at[0, :, 3 + i],
            send_sem=xsend.at[i], recv_sem=xrecv.at[i], device_id=(p, across), device_id_type=MESH,
        )

    def ycopy(n, way, kind):
        landing = 2 if kind else (3 if way == 0 else 1)
        source = 0 if kind == 0 else (3 if way == 0 else 1)
        return pltpu.make_async_remote_copy(
            src_ref=arr.at[source, :, n], dst_ref=arr.at[landing, :, n],
            send_sem=ysend.at[way, kind, n], recv_sem=yrecv.at[way, kind, n],
            device_id=(p, up if way == 0 else down), device_id_type=MESH,
        )

    def own_step(n):
        if n < 3:
            zcopies[8 + n].wait_recv()
            xcopy(n).start()
        else:
            xcopy(n - 3).wait_recv()
        ycopy(n, 0, 0).start()
        ycopy(n, 1, 0).start()

    def pass_step(n):
        ycopy(n, 0, 0).wait_recv()
        ycopy(n, 1, 0).wait_recv()
        ycopy(n, n % 2, 1).start()

    resident_chunk(0)
    own_step(0)
    resident_chunk(1)
    own_step(1)
    own_step(2)
    for j in (8, 9, 10):
        zcopies[j].wait_send()
    for j in (4, 5, 6, 7):
        zcopies[j].start()
    own_step(3)
    pass_step(0)
    own_step(4)
    own_step(5)
    w_mate.start()
    w_far.start()
    pass_step(1)
    pass_step(2)
    resident_chunk(2)
    pass_step(3)
    pass_step(4)
    pass_step(5)
    resident_chunk(3)
    resident_chunk(4)
    resident_chunk(5)
    keep.wait()
    for j in (1, 2, 3):
        zcopies[j].wait_recv()
    near_chunk(0)
    for rel in range(4):
        far_bias(rel)
    far_chunk(0)
    for j in (4, 5, 6, 7):
        zcopies[j].wait_recv()
    near_chunk(1)
    far_chunk(3)
    far_chunk(1)
    for n in range(6):
        ycopy(n, n % 2, 1).wait_recv()
    uv_load.wait()

    def hcopy(way, a, half):
        cols = pl.ds(1024 * half, 1024)
        src = 0 if a == 1 else 2 * (a - 1) - 1 + way
        dst = 7 if a == 4 else 2 * a - 1 + way
        return pltpu.make_async_remote_copy(
            src_ref=hbuf.at[src, :, cols], dst_ref=hbuf.at[dst, :, cols],
            send_sem=hsend.at[way, a - 1, half], recv_sem=hrecv.at[way, a - 1, half],
            device_id=(right if way == 0 else left, h), device_id_type=MESH,
        )

    def finish(cols):
        for two in range(cols.start // 128, (cols.start + cols.size) // 128):
            at = pl.ds(two * 128, 128)
            mixed = (acc[:, at] / l_s[:1, at]).astype(BF16).T
            for n in range(2):
                hbuf[0, :, two * 256 + n * 128 : two * 256 + (n + 1) * 128] = jnp.dot(
                    mixed[n * 64 : (n + 1) * 64], uv_v[two * 2 + n], preferred_element_type=F32
                ).astype(BF16)
        half = cols.start // 512
        hcopy(0, 1, half).start()
        hcopy(1, 1, half).start()

    far_chunk(2, tiles_of=(pl.ds(0, 512), pl.ds(512, 512)), after=finish)

    def tile_copy(slot, i, to_head):
        return pltpu.make_async_remote_copy(
            src_ref=tiles.at[slot, i], dst_ref=landed.at[h, g],
            send_sem=rsend.at[slot, i], recv_sem=rrecv.at[h, g],
            device_id=(z * 4 + lax.rem(g + i, 4), to_head), device_id_type=MESH,
        )

    def slot_head(slot):
        if slot == 0:
            return z
        if slot == 7:
            return lax.rem(z + 4, 8)
        a = (slot + 1) // 2
        return lax.rem(z + 8 - a, 8) if slot % 2 else lax.rem(z + a, 8)

    def multiply(first, count):
        lhs = hbuf[pl.ds(first, count)].reshape(64 * count, 2048)
        for i in range(4):
            part = lax.dot_general(lhs, w_v[i], NT, preferred_element_type=F32).astype(BF16)
            for n in range(count):
                slot = first + n
                to_head = slot_head(slot)
                tiles[slot, i] = part[64 * n : 64 * (n + 1)]
                copy = tile_copy(slot, i, to_head)
                if i == 0:
                    @pl.when(to_head != h)
                    def _(copy=copy):
                        copy.start()

                    @pl.when(to_head == h)
                    def _(slot=slot):
                        landed[h, g] = tiles[slot, 0]
                else:
                    copy.start()

    w_far.wait_recv()
    w_pass.start()
    w_load.wait()
    w_mate.wait_recv()
    w_pass.wait_recv()
    multiply(0, 1)
    order = [(0, 0), (1, 0), (0, 1), (1, 1)]
    for a in range(1, 4):
        for way, half in order:
            hcopy(way, a, half).wait_recv()
            if a < 3 or way == half:
                hcopy(way, a + 1, half).start()
        multiply(2 * a - 1, 2)
    hcopy(0, 4, 0).wait_recv()
    hcopy(1, 4, 1).wait_recv()
    multiply(7, 1)

    for dh in range(8):
        for i in range(4):
            if dh or i:
                hh, gg = lax.rem(h + dh, 8), lax.rem(g + i, 4)
                pltpu.make_async_remote_copy(
                    src_ref=tiles.at[0, 0], dst_ref=landed.at[hh, gg],
                    send_sem=rsend.at[0, 0], recv_sem=rrecv.at[hh, gg],
                    device_id=(z * 4 + gg, hh), device_id_type=MESH,
                ).wait_recv()
    total = landed[0].astype(F32)
    for n in range(1, 8):
        total = total + landed[n].astype(F32)
    out[...] = total.astype(BF16)

    for j in range(1, 8):
        zcopies[j].wait_send()
    for i in range(3):
        xcopy(i).wait_send()
    for n in range(6):
        ycopy(n, 0, 0).wait_send()
        ycopy(n, 1, 0).wait_send()
        ycopy(n, n % 2, 1).wait_send()
    w_mate.wait_send()
    w_far.wait_send()
    w_pass.wait_send()
    for way, half in order:
        for a in range(1, 5):
            if a < 4 or way == half:
                hcopy(way, a, half).wait_send()
    for slot in range(8):
        to_head = slot_head(slot)
        for i in range(4):
            if i == 0:
                @pl.when(to_head != h)
                def _(slot=slot, to_head=to_head):
                    tile_copy(slot, 0, to_head).wait_send()
            else:
                tile_copy(slot, i, to_head).wait_send()


ANY = pl.BlockSpec(memory_space=pl.ANY)
VMEM = pl.BlockSpec(memory_space=pltpu.VMEM)
SMEM = pl.BlockSpec(memory_space=pltpu.SMEM)
DMA = pltpu.SemaphoreType.DMA


def per_device(
    span_cache, destination, resident, block_table, lengths, new_latent, query, w_uk, w_uv, w_out
):
    table = jnp.concatenate([block_table.T, lengths[None, :], jnp.zeros((7, 16), jnp.int32)], axis=0)
    table = jnp.broadcast_to(table[:, None, :, None], (40, 2, 16, 4)).reshape(40, 128)
    out = pl.pallas_call(
        kernel,
        out_shape=jax.ShapeDtypeStruct((4, 64, 224), BF16),
        in_specs=[SMEM, VMEM] + [ANY] * 7,
        out_specs=VMEM,
        scratch_shapes=[
            pltpu.VMEM((32, 64, 576), BF16),
            pltpu.VMEM((3072, 576), BF16),
            pltpu.VMEM((16, 128, 512), BF16),
            pltpu.VMEM((16, 512, 128), BF16),
            pltpu.VMEM((16, 4, 576), BF16),
            pltpu.VMEM((1024, 192), BF16),
            pltpu.VMEM((2, 1024, 128), F32),
            pltpu.VMEM((7168, 128), F32),
            pltpu.VMEM((11, 9, 64, 128), BF16),
            pltpu.VMEM((2, 9, 4, 64, 128), BF16),
            pltpu.VMEM((4, 9, 6, 64, 128), BF16),
            pltpu.VMEM((512, 1024), BF16),
            pltpu.VMEM((128, 1024), BF16),
            pltpu.VMEM((128, 1024), BF16),
            pltpu.VMEM((512, 768), BF16),
            pltpu.VMEM((512, 1024), F32),
            pltpu.VMEM((8, 1024), F32),
            pltpu.VMEM((8, 1024), F32),
            pltpu.VMEM((4, 224, 2048), BF16),
            pltpu.VMEM((8, 64, 2048), BF16),
            pltpu.VMEM((8, 4, 64, 224), BF16),
            pltpu.VMEM((8, 4, 64, 224), BF16),
            DMA((6,)), DMA((6,)), DMA((11,)), DMA((11,)), DMA((3,)), DMA((3,)),
            DMA((2, 2, 6)), DMA((2, 2, 6)), DMA((3,)), DMA((3,)),
            DMA((2, 4, 2)), DMA((2, 4, 2)), DMA((8, 4)), DMA((8, 4)),
        ],
        compiler_params=pltpu.CompilerParams(
            collective_id=0, has_side_effects=True, vmem_limit_bytes=60 * 1024 * 1024
        ),
        name="handoff_attend_project",
    )(
        destination, table, query.reshape(1024, 192), span_cache, resident.reshape(3072, 576), new_latent,
        w_uk, w_uv, w_out.T,
    )
    return out.reshape(64, 4, 224)


def solution(mesh):
    return jax.shard_map(
        per_device,
        mesh=mesh,
        in_specs=(
            P("pool", None, None),
            P("pool", None),
            P("pool", None, None),
            P("pool", None),
            P("pool"),
            P("pool", None, None),
            P("pool", None, "head", None),
            P("head", None, None),
            P("head", None, None),
            P("head", "pool"),
        ),
        out_specs=P("head", None, "pool"),
        check_vma=False,
    )
```

```python
import functools

import jax
import jax.numpy as jnp
from jax import lax
from jax.experimental import pallas as pl
from jax.experimental.pallas import tpu as pltpu
from jax.sharding import PartitionSpec as P

MESH = pl.DeviceIdType.MESH
F32 = jnp.float32
BF16 = jnp.bfloat16
NT = (((1,), (1,)), ((), ()))
QT = 1024
SENT = (8, 9, 10, 0, 1, 2, 3, 4, 5, 6, 7)


def coords():
    p = lax.axis_index("pool")
    h = lax.axis_index("head")
    return p // 4, lax.rem(p // 2, 2), lax.rem(p, 2), h // 2, lax.rem(h, 2)


DIRECT = ((0, 0), (0, 1), (0, 2), (0, 3), (1, 0), (1, 1), (7, 0), (7, 1))


def split_offset(i, y, xh):
    dz0, k0 = (1 + 6 * (y // 2), 2 + lax.rem(y, 2)) if i == 0 else (2 * i + 1, lax.rem(y + i, 4))
    dz1, k1 = (2, 6, 4)[i], lax.rem(y + i, 4)
    return jnp.where(xh == 0, dz0, dz1), jnp.where(xh == 0, k0, k1)


def offset_of(j, y, xh):
    return DIRECT[j] if j < 8 else split_offset(j - 8, y, xh)


def peer_of(j, z, xl, c, y, xh, sign):
    dz, k = offset_of(j, y, xh)
    return pool_at(dz, k, z, xl, c, sign)


def pool_at(dz, k, z, xl, c, sign):
    return lax.rem(z + 8 + sign * dz, 8) * 4 + lax.rem(xl + k // 2, 2) * 2 + lax.rem(c + k, 2)


def kernel(
    dest, table, query, span, resident, fresh, w_uk, w_uv, w_out,
    out,
    span_v, res_v, uk_v, uv_v, fresh_v, query_v, query_f, bias_v, sendbuf, near, arr, q_main, q_low, q_high, turned,
    acc, m_s, l_s, w_v, hbuf, tiles, landed,
    load_sem, res_sem, zsend, zrecv, xsend, xrecv, ysend, yrecv, wsend, wrecv, hsend, hrecv, rsend, rrecv,
):
    z, xl, c, y, xh = coords()
    p = lax.axis_index("pool")
    h = lax.axis_index("head")
    g = lax.rem(p, 4)
    up = lax.rem(y + 1, 4) * 2 + xh
    down = lax.rem(y + 3, 4) * 2 + xh
    across = y * 2 + 1 - xh
    core_mate = p + 1 - 2 * c
    xl_mate = p + 2 - 4 * xl
    right = lax.rem(z + 1, 8) * 4 + g
    left = lax.rem(z + 7, 8) * 4 + g

    load = lambda src, dst, n: pltpu.make_async_copy(src, dst, load_sem.at[n])
    span_load = load(span, span_v, 0)
    query_load = load(query, query_v, 1)
    uk_load = load(w_uk, uk_v, 2)
    fresh_load = load(fresh, fresh_v, 3)
    uv_load = load(w_uv, uv_v, 4)
    w_load = load(w_out, w_v.at[0], 5)
    res_loads = [
        pltpu.make_async_copy(resident.at[pl.ds(512 * n, 512)], res_v.at[pl.ds(512 * n, 512)], res_sem.at[n])
        for n in range(6)
    ]
    span_load.start()

    barrier = pltpu.get_barrier_semaphore()

    def greet(pool_to, head_to):
        pl.semaphore_signal(barrier, inc=1, device_id=(pool_to, head_to), device_id_type=MESH)

    for j in range(1, 11):
        for sign in (1, -1):
            greet(peer_of(j, z, xl, c, y, xh, sign), h)
    greet(p, up)
    greet(p, down)
    greet(p, across)
    greet(core_mate, h)
    greet(xl_mate, h)
    greet(right, h)
    greet(left, h)
    for dh in range(8):
        for i in range(4):
            if dh or i:
                greet(z * 4 + lax.rem(g + i, 4), lax.rem(h + dh, 8))

    owners = [peer_of(j, z, xl, c, y, xh, 1) for j in range(11)]
    last = [jnp.int32(-1)] * 11
    first = [jnp.int32(-1)] * 11
    for b in range(32):
        ahead, behind = dest[b, 0], dest[31 - b, 0]
        for j in range(11):
            last[j] = jnp.where(ahead == owners[j], b, last[j])
            first[j] = jnp.where(behind == owners[j], 31 - b, first[j])

    span_load.wait()
    for one in [query_load, uk_load, fresh_load] + res_loads + [uv_load, w_load]:
        one.start()
    zcopies = {}
    for j in SENT:
        live = (last[j] >= 0).astype(F32).astype(BF16)
        for ab in range(2):
            block = span_v[jnp.maximum(last[j] if ab else first[j], 0)] * live
            for slab in range(4):
                sendbuf[j, ab * 4 + slab] = block[:, slab * 128 : (slab + 1) * 128]
            if ab == 0:
                low = block[:, 512:]
            else:
                sendbuf[j, 8] = jnp.concatenate([low, block[:, 512:]], axis=1)
        if j == 0:
            keep = pltpu.make_async_copy(sendbuf.at[0], near.at[0, :, 0], zrecv.at[0])
            keep.start()
            continue
        zcopies[j] = pltpu.make_async_remote_copy(
            src_ref=sendbuf.at[j],
            dst_ref=near.at[j // 4, :, j % 4] if j < 8 else arr.at[0, :, j - 8],
            send_sem=zsend.at[j],
            recv_sem=zrecv.at[j],
            device_id=(peer_of(j, z, xl, c, y, xh, 1), h), device_id_type=MESH,
        )
        if j == 8:
            pl.semaphore_wait(barrier, 58)
        if j in (8, 1, 2, 3):
            zcopies[j].start()

    def wcopy(src, owner, to, n):
        slot = lax.rem(owner - lax.rem(to, 4) + 4, 4)
        return pltpu.make_async_remote_copy(
            src_ref=src, dst_ref=w_v.at[slot], send_sem=wsend.at[n], recv_sem=wrecv.at[n],
            device_id=(to, h), device_id_type=MESH,
        )

    w_mate = wcopy(w_out, g, core_mate, 0)
    w_far = wcopy(w_out, g, xl_mate, 1)
    w_pass = wcopy(w_v.at[2], lax.rem(g + 2, 4), core_mate, 2)

    query_load.wait()
    query_f[0] = query_v[:, :128].astype(F32)
    query_f[1] = jnp.concatenate([query_v[:, 128:].astype(F32), jnp.zeros((1024, 64), F32)], axis=1)
    uk_load.wait()

    @pl.loop(0, 8)
    def _(two):
        cols = pl.ds(pl.multiple_of(two * 128, 128), 128)
        plain, rope = (
            jnp.concatenate([query_f[part, pl.ds(two * 2 + n, 64, stride=16), :] for n in range(2)], axis=0).astype(BF16)
            for part in range(2)
        )
        q_main[:, cols] = jnp.concatenate(
            [
                jnp.dot(plain[64 * n : 64 * (n + 1)], uk_v[two * 2 + n], preferred_element_type=F32)
                for n in range(2)
            ],
            axis=0,
        ).astype(BF16).T
        rope = rope.T
        q_low[:, cols] = rope
        q_high[:, cols] = jnp.concatenate([rope[64:], rope[:64]], axis=0)

    scale = 1.4426950408889634 * 192 ** -0.5

    def fold(cols, s, values, first=False):
        top = jnp.max(s, axis=0, keepdims=True)
        if not first:
            before = m_s[:1, cols]
            top = jnp.maximum(top, before)
        p_ = jnp.exp2(s - top)
        total = jnp.sum(p_, axis=0, keepdims=True)
        mix = jnp.dot(values, p_.astype(BF16), preferred_element_type=F32)
        if not first:
            fade = jnp.exp2(before - top)
            total = total + l_s[:1, cols] * fade
            mix = mix + acc[:, cols] * fade
        acc[:, cols] = mix
        m_s[:1, cols] = top
        l_s[:1, cols] = total

    fresh_load.wait()
    new = fresh_v[...].reshape(64, 576)
    turned[:, :64] = new[:, :512].T
    ALL = pl.ds(0, 1024)
    s = jnp.dot(new[:, :512], q_main[...], preferred_element_type=F32)
    s = s + jnp.dot(new[:, 512:], q_low[:64, :], preferred_element_type=F32)
    token = lax.broadcasted_iota(jnp.int32, s.shape, 0)
    lane = lax.broadcasted_iota(jnp.int32, s.shape, 1)
    seen = (((lane >> 2) & 15) == (token >> 2)) & ((lane & 3) >= (token & 3))
    fold(ALL, jnp.where(seen, s * scale, -jnp.inf), turned[:, :64], first=True)

    length = table[32:33, :]
    whole = length >> 6
    position = lax.broadcasted_iota(jnp.int32, (32, 128), 0)
    full = jnp.where(position < whole, table[:32, :], -1)
    partial = jnp.max(jnp.where(position == whole, table[:32, :], -1), axis=0, keepdims=True)
    inside = lax.broadcasted_iota(jnp.int32, (64, 128), 0) < (length & 63)

    def fill_bias(n, page):
        count = jnp.sum(jnp.where(full == page, 1.0, 0.0), axis=0, keepdims=True)
        reads = count + jnp.where(inside & (partial == page), 1.0, 0.0)
        bias_v[64 * n : 64 * (n + 1), :] = jnp.where(reads > 0, jnp.log2(jnp.maximum(reads, 1.0)), -jnp.inf)

    def fill_pairs(n, offsets):
        for ab in range(2):
            for m, (dz, k) in enumerate(offsets):
                fill_bias(n + ab * len(offsets) + m, 48 + 2 * pool_at(dz, k, z, xl, c, -1) + ab)

    def biased(s, toks, width):
        b = bias_v[toks, :]
        return s * scale + jnp.concatenate([b] * (width // 128), axis=1)

    def resident_chunk(n):
        for page in range(8 * n, 8 * n + 8):
            fill_bias(page, page)
        res_loads[n].wait()
        toks = pl.ds(512 * n, 512)
        turned[:, :512] = res_v[toks, :512].T
        s = jnp.dot(res_v[toks, :512], q_main[...], preferred_element_type=F32)
        s = s + jnp.dot(res_v[toks, 512:], q_low[:64, :], preferred_element_type=F32)
        fold(ALL, biased(s, toks, 1024), turned[:, :512])

    def arrived_chunk(held, first, count, tiles_of=(ALL,), after=None):
        half = 64 * count
        for ab in range(2):
            for j in range(4):
                turned[j * 128 : (j + 1) * 128, ab * half : (ab + 1) * half] = (
                    held[ab * 4 + j].reshape(half, 128).T
                )
        for cols in tiles_of:
            rope = held[8].reshape(half, 128)
            main = jnp.concatenate(
                [
                    jnp.concatenate([held[ab * 4 + j].reshape(half, 128) for j in range(4)], axis=1)
                    for ab in range(2)
                ],
                axis=0,
            )
            s = jnp.dot(main, q_main[:, cols], preferred_element_type=F32)
            s = s + jnp.concatenate(
                [jnp.dot(rope, q[:, cols], preferred_element_type=F32) for q in (q_low, q_high)], axis=0
            )
            fold(cols, biased(s, pl.ds(first, 2 * half), cols.size), turned[:, : 2 * half])
            if after is not None:
                after(cols)

    def near_chunk(n):
        fill_pairs(48 + 8 * n, DIRECT[4 * n : 4 * n + 4])
        arrived_chunk(near.at[n], 3072 + 512 * n, 4)

    def far_bias(rel):
        member = lax.rem(y + rel, 4)
        fill_pairs(64 + 12 * rel, [split_offset(m % 3, member, lax.rem(xh + m // 3, 2)) for m in range(6)])

    def far_chunk(rel, **how):
        arrived_chunk(arr.at[rel], 4096 + 768 * rel, 6, **how)

    def xcopy(i):
        return pltpu.make_async_remote_copy(
            src_ref=arr.at[0, :, i], dst_ref=arr.at[0, :, 3 + i],
            send_sem=xsend.at[i], recv_sem=xrecv.at[i], device_id=(p, across), device_id_type=MESH,
        )

    def ycopy(n, way, kind):
        landing = 2 if kind else (3 if way == 0 else 1)
        source = 0 if kind == 0 else (3 if way == 0 else 1)
        return pltpu.make_async_remote_copy(
            src_ref=arr.at[source, :, n], dst_ref=arr.at[landing, :, n],
            send_sem=ysend.at[way, kind, n], recv_sem=yrecv.at[way, kind, n],
            device_id=(p, up if way == 0 else down), device_id_type=MESH,
        )

    def own_step(n):
        if n < 3:
            zcopies[8 + n].wait_recv()
            xcopy(n).start()
        else:
            xcopy(n - 3).wait_recv()
        ycopy(n, 0, 0).start()
        ycopy(n, 1, 0).start()

    def pass_step(n):
        ycopy(n, 0, 0).wait_recv()
        ycopy(n, 1, 0).wait_recv()
        ycopy(n, n % 2, 1).start()

    zcopies[9].start()
    zcopies[10].start()
    resident_chunk(0)
    own_step(0)
    resident_chunk(1)
    own_step(1)
    own_step(2)
    for j in (4, 5, 6, 7):
        zcopies[j].start()
    w_mate.start()
    w_far.start()
    own_step(3)
    pass_step(0)
    own_step(4)
    own_step(5)
    pass_step(1)
    resident_chunk(2)
    pass_step(2)
    resident_chunk(3)
    pass_step(3)
    resident_chunk(4)
    pass_step(4)
    resident_chunk(5)
    keep.wait()
    for j in (1, 2, 3):
        zcopies[j].wait_recv()
    near_chunk(0)
    pass_step(5)
    for rel in range(4):
        far_bias(rel)
    far_chunk(0)
    for j in (4, 5, 6, 7):
        zcopies[j].wait_recv()
    near_chunk(1)
    far_chunk(3)
    far_chunk(1)
    w_far.wait_recv()
    w_pass.start()
    for n in range(6):
        ycopy(n, n % 2, 1).wait_recv()
    uv_load.wait()

    def hcopy(way, a, half):
        cols = pl.ds(1024 * half, 1024)
        src = 0 if a == 1 else 2 * (a - 1) - 1 + way
        dst = 7 if a == 4 else 2 * a - 1 + way
        return pltpu.make_async_remote_copy(
            src_ref=hbuf.at[src, :, cols], dst_ref=hbuf.at[dst, :, cols],
            send_sem=hsend.at[way, a - 1, half], recv_sem=hrecv.at[way, a - 1, half],
            device_id=(right if way == 0 else left, h), device_id_type=MESH,
        )

    def finish(cols):
        for two in range(cols.start // 128, (cols.start + cols.size) // 128):
            at = pl.ds(two * 128, 128)
            mixed = (acc[:, at] / l_s[:1, at]).astype(BF16).T
            for n in range(2):
                hbuf[0, :, two * 256 + n * 128 : two * 256 + (n + 1) * 128] = jnp.dot(
                    mixed[n * 64 : (n + 1) * 64], uv_v[two * 2 + n], preferred_element_type=F32
                ).astype(BF16)
        half = cols.start // 512
        hcopy(0, 1, half).start()
        hcopy(1, 1, half).start()

    far_chunk(2, tiles_of=(pl.ds(0, 512), pl.ds(512, 512)), after=finish)

    def tile_copy(slot, i, to_head):
        return pltpu.make_async_remote_copy(
            src_ref=tiles.at[slot, i], dst_ref=landed.at[h, g],
            send_sem=rsend.at[slot, i], recv_sem=rrecv.at[h, g],
            device_id=(z * 4 + lax.rem(g + i, 4), to_head), device_id_type=MESH,
        )

    def slot_head(slot):
        if slot == 0:
            return z
        if slot == 7:
            return lax.rem(z + 4, 8)
        a = (slot + 1) // 2
        return lax.rem(z + 8 - a, 8) if slot % 2 else lax.rem(z + a, 8)

    def multiply(first, count):
        lhs = hbuf[pl.ds(first, count)].reshape(64 * count, 2048)
        for i in range(4):
            part = lax.dot_general(lhs, w_v[i], NT, preferred_element_type=F32).astype(BF16)
            for n in range(count):
                slot = first + n
                to_head = slot_head(slot)
                tiles[slot, i] = part[64 * n : 64 * (n + 1)]
                copy = tile_copy(slot, i, to_head)
                if i == 0:
                    @pl.when(to_head != h)
                    def _(copy=copy):
                        copy.start()

                    @pl.when(to_head == h)
                    def _(slot=slot):
                        landed[h, g] = tiles[slot, 0]
                else:
                    copy.start()

    order = [(0, 0), (1, 0), (0, 1), (1, 1)]
    for a in range(1, 4):
        for way, half in order:
            hcopy(way, a, half).wait_recv()
            if a < 3 or way == half:
                hcopy(way, a + 1, half).start()
        if a == 1:
            w_load.wait()
            w_mate.wait_recv()
            w_pass.wait_recv()
            multiply(0, 3)
        else:
            multiply(2 * a - 1, 2)
    hcopy(0, 4, 0).wait_recv()
    hcopy(1, 4, 1).wait_recv()
    multiply(7, 1)

    for dh in range(8):
        for i in range(4):
            if dh or i:
                hh, gg = lax.rem(h + dh, 8), lax.rem(g + i, 4)
                pltpu.make_async_remote_copy(
                    src_ref=tiles.at[0, 0], dst_ref=landed.at[hh, gg],
                    send_sem=rsend.at[0, 0], recv_sem=rrecv.at[hh, gg],
                    device_id=(z * 4 + gg, hh), device_id_type=MESH,
                ).wait_recv()
    total = landed[0].astype(F32)
    for n in range(1, 8):
        total = total + landed[n].astype(F32)
    out[...] = total.astype(BF16)

    for j in range(1, 11):
        zcopies[j].wait_send()
    for i in range(3):
        xcopy(i).wait_send()
    for n in range(6):
        ycopy(n, 0, 0).wait_send()
        ycopy(n, 1, 0).wait_send()
        ycopy(n, n % 2, 1).wait_send()
    w_mate.wait_send()
    w_far.wait_send()
    w_pass.wait_send()
    for way, half in order:
        for a in range(1, 5):
            if a < 4 or way == half:
                hcopy(way, a, half).wait_send()
    for slot in range(8):
        to_head = slot_head(slot)
        for i in range(4):
            if i == 0:
                @pl.when(to_head != h)
                def _(slot=slot, to_head=to_head):
                    tile_copy(slot, 0, to_head).wait_send()
            else:
                tile_copy(slot, i, to_head).wait_send()


ANY = pl.BlockSpec(memory_space=pl.ANY)
VMEM = pl.BlockSpec(memory_space=pltpu.VMEM)
SMEM = pl.BlockSpec(memory_space=pltpu.SMEM)
DMA = pltpu.SemaphoreType.DMA


def per_device(
    span_cache, destination, resident, block_table, lengths, new_latent, query, w_uk, w_uv, w_out
):
    table = jnp.concatenate([block_table.T, lengths[None, :], jnp.zeros((7, 16), jnp.int32)], axis=0)
    table = jnp.broadcast_to(table[:, None, :, None], (40, 2, 16, 4)).reshape(40, 128)
    out = pl.pallas_call(
        kernel,
        out_shape=jax.ShapeDtypeStruct((4, 64, 224), BF16),
        in_specs=[SMEM, VMEM] + [ANY] * 7,
        out_specs=VMEM,
        scratch_shapes=[
            pltpu.VMEM((32, 64, 576), BF16),
            pltpu.VMEM((3072, 576), BF16),
            pltpu.VMEM((16, 128, 512), BF16),
            pltpu.VMEM((16, 512, 128), BF16),
            pltpu.VMEM((16, 4, 576), BF16),
            pltpu.VMEM((1024, 192), BF16),
            pltpu.VMEM((2, 1024, 128), F32),
            pltpu.VMEM((7168, 128), F32),
            pltpu.VMEM((11, 9, 64, 128), BF16),
            pltpu.VMEM((2, 9, 4, 64, 128), BF16),
            pltpu.VMEM((4, 9, 6, 64, 128), BF16),
            pltpu.VMEM((512, 1024), BF16),
            pltpu.VMEM((128, 1024), BF16),
            pltpu.VMEM((128, 1024), BF16),
            pltpu.VMEM((512, 768), BF16),
            pltpu.VMEM((512, 1024), F32),
            pltpu.VMEM((8, 1024), F32),
            pltpu.VMEM((8, 1024), F32),
            pltpu.VMEM((4, 224, 2048), BF16),
            pltpu.VMEM((8, 64, 2048), BF16),
            pltpu.VMEM((8, 4, 64, 224), BF16),
            pltpu.VMEM((8, 4, 64, 224), BF16),
            DMA((6,)), DMA((6,)), DMA((11,)), DMA((11,)), DMA((3,)), DMA((3,)),
            DMA((2, 2, 6)), DMA((2, 2, 6)), DMA((3,)), DMA((3,)),
            DMA((2, 4, 2)), DMA((2, 4, 2)), DMA((8, 4)), DMA((8, 4)),
        ],
        compiler_params=pltpu.CompilerParams(
            collective_id=0, has_side_effects=True, vmem_limit_bytes=60 * 1024 * 1024
        ),
        name="handoff_attend_project",
    )(
        destination, table, query.reshape(1024, 192), span_cache, resident.reshape(3072, 576), new_latent,
        w_uk, w_uv, w_out.T,
    )
    return out.reshape(64, 4, 224)


def solution(mesh):
    return jax.shard_map(
        per_device,
        mesh=mesh,
        in_specs=(
            P("pool", None, None),
            P("pool", None),
            P("pool", None, None),
            P("pool", None),
            P("pool"),
            P("pool", None, None),
            P("pool", None, "head", None),
            P("head", None, None),
            P("head", None, None),
            P("head", "pool"),
        ),
        out_specs=P("head", None, "pool"),
        check_vma=False,
    )
```

```python
import functools

import jax
import jax.numpy as jnp
from jax import lax
from jax.experimental import pallas as pl
from jax.experimental.pallas import tpu as pltpu
from jax.sharding import PartitionSpec as P

MESH = pl.DeviceIdType.MESH
F32 = jnp.float32
BF16 = jnp.bfloat16
NT = (((1,), (1,)), ((), ()))
QT = 1024
SENT = (8, 9, 10, 0, 1, 2, 3, 4, 5, 6, 7)


def coords():
    p = lax.axis_index("pool")
    h = lax.axis_index("head")
    return p // 4, lax.rem(p // 2, 2), lax.rem(p, 2), h // 2, lax.rem(h, 2)


DIRECT = ((0, 0), (0, 1), (0, 2), (0, 3), (1, 0), (1, 1), (7, 0), (7, 1))


def split_offset(i, y, xh):
    dz0, k0 = (1 + 6 * (y // 2), 2 + lax.rem(y, 2)) if i == 0 else (2 * i + 1, lax.rem(y + i, 4))
    dz1, k1 = (2, 6, 4)[i], lax.rem(y + i, 4)
    return jnp.where(xh == 0, dz0, dz1), jnp.where(xh == 0, k0, k1)


def offset_of(j, y, xh):
    return DIRECT[j] if j < 8 else split_offset(j - 8, y, xh)


def peer_of(j, z, xl, c, y, xh, sign):
    dz, k = offset_of(j, y, xh)
    return pool_at(dz, k, z, xl, c, sign)


def pool_at(dz, k, z, xl, c, sign):
    return lax.rem(z + 8 + sign * dz, 8) * 4 + lax.rem(xl + k // 2, 2) * 2 + lax.rem(c + k, 2)


def kernel(
    given, query, span, resident, fresh, w_uk, w_uv, w_out,
    out,
    dest, table, span_v, res_v, uk_v, uv_v, fresh_v, query_v, query_f, bias_v, sendbuf, near, arr, q_main, q_low, q_high, turned,
    acc, m_s, l_s, w_v, hbuf, tiles, landed,
    load_sem, res_sem, zsend, zrecv, xsend, xrecv, ysend, yrecv, wsend, wrecv, hsend, hrecv, rsend, rrecv,
):
    z, xl, c, y, xh = coords()
    p = lax.axis_index("pool")
    h = lax.axis_index("head")
    g = lax.rem(p, 4)
    up = lax.rem(y + 1, 4) * 2 + xh
    down = lax.rem(y + 3, 4) * 2 + xh
    across = y * 2 + 1 - xh
    core_mate = p + 1 - 2 * c
    xl_mate = p + 2 - 4 * xl
    right = lax.rem(z + 1, 8) * 4 + g
    left = lax.rem(z + 7, 8) * 4 + g

    load = lambda src, dst, n: pltpu.make_async_copy(src, dst, load_sem.at[n])
    span_load = load(span, span_v, 0)
    query_load = load(query, query_v, 1)
    uk_load = load(w_uk, uk_v, 2)
    fresh_load = load(fresh, fresh_v, 3)
    uv_load = load(w_uv, uv_v, 4)
    w_load = load(w_out, w_v.at[0], 5)
    res_loads = [
        pltpu.make_async_copy(resident.at[pl.ds(512 * n, 512)], res_v.at[pl.ds(512 * n, 512)], res_sem.at[n])
        for n in range(6)
    ]
    table_load = load(given, table, 6)
    dest_load = load(given.at[pl.ds(32, 8)], dest, 7)
    dest_load.start()
    span_load.start()
    table_load.start()

    barrier = pltpu.get_barrier_semaphore()

    def greet(pool_to, head_to):
        pl.semaphore_signal(barrier, inc=1, device_id=(pool_to, head_to), device_id_type=MESH)

    for j in range(1, 11):
        for sign in (1, -1):
            greet(peer_of(j, z, xl, c, y, xh, sign), h)
    greet(p, up)
    greet(p, down)
    greet(p, across)
    greet(core_mate, h)
    greet(xl_mate, h)
    greet(right, h)
    greet(left, h)
    for dh in range(8):
        for i in range(4):
            if dh or i:
                greet(z * 4 + lax.rem(g + i, 4), lax.rem(h + dh, 8))

    owners = [peer_of(j, z, xl, c, y, xh, 1) for j in range(11)]
    last = [jnp.int32(-1)] * 11
    dest_load.wait()
    first = [jnp.int32(-1)] * 11
    for b in range(32):
        ahead, behind = dest[1, b], dest[1, 31 - b]
        for j in range(11):
            last[j] = jnp.where(ahead == owners[j], b, last[j])
            first[j] = jnp.where(behind == owners[j], 31 - b, first[j])

    span_load.wait()
    for one in [query_load, uk_load, fresh_load] + res_loads + [uv_load, w_load]:
        one.start()
    zcopies = {}
    for j in SENT:
        live = (last[j] >= 0).astype(F32).astype(BF16)
        for ab in range(2):
            block = span_v[jnp.maximum(last[j] if ab else first[j], 0)] * live
            for slab in range(4):
                sendbuf[j, ab * 4 + slab] = block[:, slab * 128 : (slab + 1) * 128]
            if ab == 0:
                low = block[:, 512:]
            else:
                sendbuf[j, 8] = jnp.concatenate([low, block[:, 512:]], axis=1)
        if j == 0:
            keep = pltpu.make_async_copy(sendbuf.at[0], near.at[0, :, 0], zrecv.at[0])
            keep.start()
            continue
        zcopies[j] = pltpu.make_async_remote_copy(
            src_ref=sendbuf.at[j],
            dst_ref=near.at[j // 4, :, j % 4] if j < 8 else arr.at[0, :, j - 8],
            send_sem=zsend.at[j],
            recv_sem=zrecv.at[j],
            device_id=(peer_of(j, z, xl, c, y, xh, 1), h), device_id_type=MESH,
        )
        if j == 8:
            pl.semaphore_wait(barrier, 58)
        if j in (8, 1, 2, 3):
            zcopies[j].start()

    def wcopy(src, owner, to, n):
        slot = lax.rem(owner - lax.rem(to, 4) + 4, 4)
        return pltpu.make_async_remote_copy(
            src_ref=src, dst_ref=w_v.at[slot], send_sem=wsend.at[n], recv_sem=wrecv.at[n],
            device_id=(to, h), device_id_type=MESH,
        )

    w_mate = wcopy(w_out, g, core_mate, 0)
    w_far = wcopy(w_out, g, xl_mate, 1)
    w_pass = wcopy(w_v.at[2], lax.rem(g + 2, 4), core_mate, 2)

    query_load.wait()
    query_f[0] = query_v[:, :128].astype(F32)
    query_f[1] = jnp.concatenate([query_v[:, 128:].astype(F32), jnp.zeros((1024, 64), F32)], axis=1)
    uk_load.wait()

    @pl.loop(0, 8)
    def _(two):
        cols = pl.ds(pl.multiple_of(two * 128, 128), 128)
        plain, rope = (
            jnp.concatenate([query_f[part, pl.ds(two * 2 + n, 64, stride=16), :] for n in range(2)], axis=0).astype(BF16)
            for part in range(2)
        )
        q_main[:, cols] = jnp.concatenate(
            [
                jnp.dot(plain[64 * n : 64 * (n + 1)], uk_v[two * 2 + n], preferred_element_type=F32)
                for n in range(2)
            ],
            axis=0,
        ).astype(BF16).T
        rope = rope.T
        q_low[:, cols] = rope
        q_high[:, cols] = jnp.concatenate([rope[64:], rope[:64]], axis=0)

    scale = 1.4426950408889634 * 192 ** -0.5

    def fold(cols, s, values, first=False):
        top = jnp.max(s, axis=0, keepdims=True)
        if not first:
            before = m_s[:1, cols]
            top = jnp.maximum(top, before)
        p_ = jnp.exp2(s - top)
        total = jnp.sum(p_, axis=0, keepdims=True)
        mix = jnp.dot(values, p_.astype(BF16), preferred_element_type=F32)
        if not first:
            fade = jnp.exp2(before - top)
            total = total + l_s[:1, cols] * fade
            mix = mix + acc[:, cols] * fade
        acc[:, cols] = mix
        m_s[:1, cols] = top
        l_s[:1, cols] = total

    fresh_load.wait()
    new = fresh_v[...].reshape(64, 576)
    turned[:, :64] = new[:, :512].T
    ALL = pl.ds(0, 1024)
    s = jnp.dot(new[:, :512], q_main[...], preferred_element_type=F32)
    s = s + jnp.dot(new[:, 512:], q_low[:64, :], preferred_element_type=F32)
    token = lax.broadcasted_iota(jnp.int32, s.shape, 0)
    lane = lax.broadcasted_iota(jnp.int32, s.shape, 1)
    seen = (((lane >> 2) & 15) == (token >> 2)) & ((lane & 3) >= (token & 3))
    fold(ALL, jnp.where(seen, s * scale, -jnp.inf), turned[:, :64], first=True)

    table_load.wait()
    length = table[32:33, :]
    whole = length >> 6
    position = lax.broadcasted_iota(jnp.int32, (32, 128), 0)
    full = jnp.where(position < whole, table[:32, :], -1)
    partial = jnp.max(jnp.where(position == whole, table[:32, :], -1), axis=0, keepdims=True)
    inside = lax.broadcasted_iota(jnp.int32, (64, 128), 0) < (length & 63)

    def fill_bias(n, page):
        count = jnp.sum(jnp.where(full == page, 1.0, 0.0), axis=0, keepdims=True)
        reads = count + jnp.where(inside & (partial == page), 1.0, 0.0)
        bias_v[64 * n : 64 * (n + 1), :] = jnp.where(reads > 0, jnp.log2(jnp.maximum(reads, 1.0)), -jnp.inf)

    def fill_pairs(n, offsets):
        for ab in range(2):
            for m, (dz, k) in enumerate(offsets):
                fill_bias(n + ab * len(offsets) + m, 48 + 2 * pool_at(dz, k, z, xl, c, -1) + ab)

    def biased(s, toks, width):
        b = bias_v[toks, :]
        return s * scale + jnp.concatenate([b] * (width // 128), axis=1)

    def resident_chunk(n):
        for page in range(8 * n, 8 * n + 8):
            fill_bias(page, page)
        res_loads[n].wait()
        toks = pl.ds(512 * n, 512)
        turned[:, :512] = res_v[toks, :512].T
        s = jnp.dot(res_v[toks, :512], q_main[...], preferred_element_type=F32)
        s = s + jnp.dot(res_v[toks, 512:], q_low[:64, :], preferred_element_type=F32)
        fold(ALL, biased(s, toks, 1024), turned[:, :512])

    def arrived_chunk(held, first, count, tiles_of=(ALL,), after=None):
        half = 64 * count
        for ab in range(2):
            for j in range(4):
                turned[j * 128 : (j + 1) * 128, ab * half : (ab + 1) * half] = (
                    held[ab * 4 + j].reshape(half, 128).T
                )
        for cols in tiles_of:
            rope = held[8].reshape(half, 128)
            main = jnp.concatenate(
                [
                    jnp.concatenate([held[ab * 4 + j].reshape(half, 128) for j in range(4)], axis=1)
                    for ab in range(2)
                ],
                axis=0,
            )
            s = jnp.dot(main, q_main[:, cols], preferred_element_type=F32)
            s = s + jnp.concatenate(
                [jnp.dot(rope, q[:, cols], preferred_element_type=F32) for q in (q_low, q_high)], axis=0
            )
            fold(cols, biased(s, pl.ds(first, 2 * half), cols.size), turned[:, : 2 * half])
            if after is not None:
                after(cols)

    def near_chunk(n):
        fill_pairs(48 + 8 * n, DIRECT[4 * n : 4 * n + 4])
        arrived_chunk(near.at[n], 3072 + 512 * n, 4)

    def far_bias(rel):
        member = lax.rem(y + rel, 4)
        fill_pairs(64 + 12 * rel, [split_offset(m % 3, member, lax.rem(xh + m // 3, 2)) for m in range(6)])

    def far_chunk(rel, **how):
        arrived_chunk(arr.at[rel], 4096 + 768 * rel, 6, **how)

    def xcopy(i):
        return pltpu.make_async_remote_copy(
            src_ref=arr.at[0, :, i], dst_ref=arr.at[0, :, 3 + i],
            send_sem=xsend.at[i], recv_sem=xrecv.at[i], device_id=(p, across), device_id_type=MESH,
        )

    def ycopy(n, way, kind):
        landing = 2 if kind else (3 if way == 0 else 1)
        source = 0 if kind == 0 else (3 if way == 0 else 1)
        return pltpu.make_async_remote_copy(
            src_ref=arr.at[source, :, n], dst_ref=arr.at[landing, :, n],
            send_sem=ysend.at[way, kind, n], recv_sem=yrecv.at[way, kind, n],
            device_id=(p, up if way == 0 else down), device_id_type=MESH,
        )

    def own_step(n):
        if n < 3:
            zcopies[8 + n].wait_recv()
            xcopy(n).start()
        else:
            xcopy(n - 3).wait_recv()
        ycopy(n, 0, 0).start()
        ycopy(n, 1, 0).start()

    def pass_step(n):
        ycopy(n, 0, 0).wait_recv()
        ycopy(n, 1, 0).wait_recv()
        ycopy(n, n % 2, 1).start()

    zcopies[9].start()
    zcopies[10].start()
    resident_chunk(0)
    own_step(0)
    resident_chunk(1)
    own_step(1)
    own_step(2)
    for j in (4, 5, 6, 7):
        zcopies[j].start()
    w_mate.start()
    w_far.start()
    own_step(3)
    pass_step(0)
    own_step(4)
    own_step(5)
    pass_step(1)
    resident_chunk(2)
    pass_step(2)
    resident_chunk(3)
    pass_step(3)
    resident_chunk(4)
    pass_step(4)
    resident_chunk(5)
    keep.wait()
    for j in (1, 2, 3):
        zcopies[j].wait_recv()
    near_chunk(0)
    pass_step(5)
    for rel in range(4):
        far_bias(rel)
    far_chunk(0)
    for j in (4, 5, 6, 7):
        zcopies[j].wait_recv()
    near_chunk(1)
    far_chunk(3)
    far_chunk(1)
    w_far.wait_recv()
    w_pass.start()
    for n in range(6):
        ycopy(n, n % 2, 1).wait_recv()
    uv_load.wait()

    def hcopy(way, a, half):
        cols = pl.ds(1024 * half, 1024)
        src = 0 if a == 1 else 2 * (a - 1) - 1 + way
        dst = 7 if a == 4 else 2 * a - 1 + way
        return pltpu.make_async_remote_copy(
            src_ref=hbuf.at[src, :, cols], dst_ref=hbuf.at[dst, :, cols],
            send_sem=hsend.at[way, a - 1, half], recv_sem=hrecv.at[way, a - 1, half],
            device_id=(right if way == 0 else left, h), device_id_type=MESH,
        )

    def finish(cols):
        for two in range(cols.start // 128, (cols.start + cols.size) // 128):
            at = pl.ds(two * 128, 128)
            mixed = (acc[:, at] / l_s[:1, at]).astype(BF16).T
            for n in range(2):
                hbuf[0, :, two * 256 + n * 128 : two * 256 + (n + 1) * 128] = jnp.dot(
                    mixed[n * 64 : (n + 1) * 64], uv_v[two * 2 + n], preferred_element_type=F32
                ).astype(BF16)
        half = cols.start // 512
        hcopy(0, 1, half).start()
        hcopy(1, 1, half).start()

    far_chunk(2, tiles_of=(pl.ds(0, 512), pl.ds(512, 512)), after=finish)

    def tile_copy(slot, i, to_head):
        return pltpu.make_async_remote_copy(
            src_ref=tiles.at[slot, i], dst_ref=landed.at[h, g],
            send_sem=rsend.at[slot, i], recv_sem=rrecv.at[h, g],
            device_id=(z * 4 + lax.rem(g + i, 4), to_head), device_id_type=MESH,
        )

    def slot_head(slot):
        if slot == 0:
            return z
        if slot == 7:
            return lax.rem(z + 4, 8)
        a = (slot + 1) // 2
        return lax.rem(z + 8 - a, 8) if slot % 2 else lax.rem(z + a, 8)

    def multiply(first, count):
        lhs = hbuf[pl.ds(first, count)].reshape(64 * count, 2048)
        for i in range(4):
            part = lax.dot_general(lhs, w_v[i], NT, preferred_element_type=F32).astype(BF16)
            for n in range(count):
                slot = first + n
                to_head = slot_head(slot)
                tiles[slot, i] = part[64 * n : 64 * (n + 1)]
                copy = tile_copy(slot, i, to_head)
                if i == 0:
                    @pl.when(to_head != h)
                    def _(copy=copy):
                        copy.start()

                    @pl.when(to_head == h)
                    def _(slot=slot):
                        landed[h, g] = tiles[slot, 0]
                else:
                    copy.start()

    order = [(0, 0), (1, 0), (0, 1), (1, 1)]
    for a in range(1, 4):
        for way, half in order:
            hcopy(way, a, half).wait_recv()
            if a < 3 or way == half:
                hcopy(way, a + 1, half).start()
        if a == 1:
            w_load.wait()
            w_mate.wait_recv()
            w_pass.wait_recv()
            multiply(0, 3)
        else:
            multiply(2 * a - 1, 2)
    hcopy(0, 4, 0).wait_recv()
    hcopy(1, 4, 1).wait_recv()
    multiply(7, 1)

    for dh in range(8):
        for i in range(4):
            if dh or i:
                hh, gg = lax.rem(h + dh, 8), lax.rem(g + i, 4)
                pltpu.make_async_remote_copy(
                    src_ref=tiles.at[0, 0], dst_ref=landed.at[hh, gg],
                    send_sem=rsend.at[0, 0], recv_sem=rrecv.at[hh, gg],
                    device_id=(z * 4 + gg, hh), device_id_type=MESH,
                ).wait_recv()
    total = landed[0].astype(F32)
    for n in range(1, 8):
        total = total + landed[n].astype(F32)
    out[...] = total.astype(BF16)

    for j in range(1, 11):
        zcopies[j].wait_send()
    for i in range(3):
        xcopy(i).wait_send()
    for n in range(6):
        ycopy(n, 0, 0).wait_send()
        ycopy(n, 1, 0).wait_send()
        ycopy(n, n % 2, 1).wait_send()
    w_mate.wait_send()
    w_far.wait_send()
    w_pass.wait_send()
    for way, half in order:
        for a in range(1, 5):
            if a < 4 or way == half:
                hcopy(way, a, half).wait_send()
    for slot in range(8):
        to_head = slot_head(slot)
        for i in range(4):
            if i == 0:
                @pl.when(to_head != h)
                def _(slot=slot, to_head=to_head):
                    tile_copy(slot, 0, to_head).wait_send()
            else:
                tile_copy(slot, i, to_head).wait_send()


ANY = pl.BlockSpec(memory_space=pl.ANY)
VMEM = pl.BlockSpec(memory_space=pltpu.VMEM)
SMEM = pl.BlockSpec(memory_space=pltpu.SMEM)
DMA = pltpu.SemaphoreType.DMA


def per_device(
    span_cache, destination, resident, block_table, lengths, new_latent, query, w_uk, w_uv, w_out
):
    table = jnp.concatenate([block_table.T, lengths[None, :]], axis=0)
    table = jnp.broadcast_to(table[:, None, :, None], (33, 2, 16, 4)).reshape(33, 128)
    owners = jnp.pad(destination.reshape(1, 32), ((0, 6), (0, 96)))
    given = jnp.concatenate([table, owners], axis=0)
    out = pl.pallas_call(
        kernel,
        out_shape=jax.ShapeDtypeStruct((4, 64, 224), BF16),
        in_specs=[ANY] * 8,
        out_specs=VMEM,
        scratch_shapes=[
            pltpu.SMEM((8, 128), jnp.int32),
            pltpu.VMEM((40, 128), jnp.int32),
            pltpu.VMEM((32, 64, 576), BF16),
            pltpu.VMEM((3072, 576), BF16),
            pltpu.VMEM((16, 128, 512), BF16),
            pltpu.VMEM((16, 512, 128), BF16),
            pltpu.VMEM((16, 4, 576), BF16),
            pltpu.VMEM((1024, 192), BF16),
            pltpu.VMEM((2, 1024, 128), F32),
            pltpu.VMEM((7168, 128), F32),
            pltpu.VMEM((11, 9, 64, 128), BF16),
            pltpu.VMEM((2, 9, 4, 64, 128), BF16),
            pltpu.VMEM((4, 9, 6, 64, 128), BF16),
            pltpu.VMEM((512, 1024), BF16),
            pltpu.VMEM((128, 1024), BF16),
            pltpu.VMEM((128, 1024), BF16),
            pltpu.VMEM((512, 768), BF16),
            pltpu.VMEM((512, 1024), F32),
            pltpu.VMEM((8, 1024), F32),
            pltpu.VMEM((8, 1024), F32),
            pltpu.VMEM((4, 224, 2048), BF16),
            pltpu.VMEM((8, 64, 2048), BF16),
            pltpu.VMEM((8, 4, 64, 224), BF16),
            pltpu.VMEM((8, 4, 64, 224), BF16),
            DMA((8,)), DMA((6,)), DMA((11,)), DMA((11,)), DMA((3,)), DMA((3,)),
            DMA((2, 2, 6)), DMA((2, 2, 6)), DMA((3,)), DMA((3,)),
            DMA((2, 4, 2)), DMA((2, 4, 2)), DMA((8, 4)), DMA((8, 4)),
        ],
        compiler_params=pltpu.CompilerParams(
            collective_id=0, has_side_effects=True, vmem_limit_bytes=60 * 1024 * 1024
        ),
        name="handoff_attend_project",
    )(
        given, query.reshape(1024, 192), span_cache, resident.reshape(3072, 576), new_latent,
        w_uk, w_uv, w_out.T,
    )
    return out.reshape(64, 4, 224)


def solution(mesh):
    return jax.shard_map(
        per_device,
        mesh=mesh,
        in_specs=(
            P("pool", None, None),
            P("pool", None),
            P("pool", None, None),
            P("pool", None),
            P("pool"),
            P("pool", None, None),
            P("pool", None, "head", None),
            P("head", None, None),
            P("head", None, None),
            P("head", "pool"),
        ),
        out_specs=P("head", None, "pool"),
        check_vma=False,
    )
```

```python
import functools

import jax
import jax.numpy as jnp
from jax import lax
from jax.experimental import pallas as pl
from jax.experimental.pallas import tpu as pltpu
from jax.sharding import PartitionSpec as P

MESH = pl.DeviceIdType.MESH
F32 = jnp.float32
BF16 = jnp.bfloat16
NT = (((1,), (1,)), ((), ()))
QT = 1024
SENT = (8, 9, 10, 0, 1, 2, 3, 4, 5, 6, 7)


def coords():
    p = lax.axis_index("pool")
    h = lax.axis_index("head")
    return p // 4, lax.rem(p // 2, 2), lax.rem(p, 2), h // 2, lax.rem(h, 2)


DIRECT = ((0, 0), (0, 1), (0, 2), (0, 3), (1, 0), (1, 1), (7, 0), (7, 1))


def split_offset(i, y, xh):
    dz0, k0 = (1 + 6 * (y // 2), 2 + lax.rem(y, 2)) if i == 0 else (2 * i + 1, lax.rem(y + i, 4))
    dz1, k1 = (2, 6, 4)[i], lax.rem(y + i, 4)
    return jnp.where(xh == 0, dz0, dz1), jnp.where(xh == 0, k0, k1)


def offset_of(j, y, xh):
    return DIRECT[j] if j < 8 else split_offset(j - 8, y, xh)


def peer_of(j, z, xl, c, y, xh, sign):
    dz, k = offset_of(j, y, xh)
    return pool_at(dz, k, z, xl, c, sign)


def pool_at(dz, k, z, xl, c, sign):
    return lax.rem(z + 8 + sign * dz, 8) * 4 + lax.rem(xl + k // 2, 2) * 2 + lax.rem(c + k, 2)


def kernel(
    given, query, span, resident, fresh, w_uk, w_uv, w_out,
    out,
    dest, table, span_v, res_v, uk_v, uv_v, fresh_v, query_v, query_f, bias_v, sendbuf, near, arr, q_main, q_low, q_high, turned,
    acc, m_s, l_s, w_v, hbuf, tiles, landed,
    load_sem, res_sem, zsend, zrecv, xsend, xrecv, ysend, yrecv, wsend, wrecv, hsend, hrecv, rsend, rrecv,
):
    z, xl, c, y, xh = coords()
    p = lax.axis_index("pool")
    h = lax.axis_index("head")
    g = lax.rem(p, 4)
    up = lax.rem(y + 1, 4) * 2 + xh
    down = lax.rem(y + 3, 4) * 2 + xh
    across = y * 2 + 1 - xh
    core_mate = p + 1 - 2 * c
    xl_mate = p + 2 - 4 * xl
    right = lax.rem(z + 1, 8) * 4 + g
    left = lax.rem(z + 7, 8) * 4 + g

    load = lambda src, dst, n: pltpu.make_async_copy(src, dst, load_sem.at[n])
    span_load = load(span, span_v, 0)
    query_load = load(query, query_v, 1)
    uk_load = load(w_uk, uk_v, 2)
    fresh_load = load(fresh, fresh_v, 3)
    uv_load = load(w_uv, uv_v, 4)
    w_load = load(w_out, w_v.at[0], 5)
    res_loads = [
        pltpu.make_async_copy(resident.at[pl.ds(512 * n, 512)], res_v.at[pl.ds(512 * n, 512)], res_sem.at[n])
        for n in range(6)
    ]
    table_load = load(given, table, 6)
    dest_load = load(given.at[pl.ds(32, 8)], dest, 7)
    dest_load.start()
    span_load.start()
    table_load.start()

    barrier = pltpu.get_barrier_semaphore()

    def greet(pool_to, head_to):
        pl.semaphore_signal(barrier, inc=1, device_id=(pool_to, head_to), device_id_type=MESH)

    for j in range(1, 11):
        for sign in (1, -1):
            greet(peer_of(j, z, xl, c, y, xh, sign), h)
    greet(p, up)
    greet(p, down)
    greet(p, across)
    greet(core_mate, h)
    greet(xl_mate, h)
    greet(right, h)
    greet(left, h)
    for dh in range(8):
        for i in range(4):
            if dh or i:
                greet(z * 4 + lax.rem(g + i, 4), lax.rem(h + dh, 8))

    owners = [peer_of(j, z, xl, c, y, xh, 1) for j in range(11)]
    last = [jnp.int32(-1)] * 11
    dest_load.wait()
    first = [jnp.int32(-1)] * 11
    for b in range(32):
        ahead, behind = dest[1, b], dest[1, 31 - b]
        for j in range(11):
            last[j] = jnp.where(ahead == owners[j], b, last[j])
            first[j] = jnp.where(behind == owners[j], 31 - b, first[j])

    span_load.wait()
    for one in [query_load, uk_load, fresh_load] + res_loads + [uv_load, w_load]:
        one.start()
    zcopies = {}
    for j in SENT:
        live = (last[j] >= 0).astype(F32).astype(BF16)
        for ab in range(2):
            block = span_v[jnp.maximum(last[j] if ab else first[j], 0)] * live
            for slab in range(4):
                sendbuf[j, ab * 4 + slab] = block[:, slab * 128 : (slab + 1) * 128]
            if ab == 0:
                low = block[:, 512:]
            else:
                sendbuf[j, 8] = jnp.concatenate([low, block[:, 512:]], axis=1)
        if j == 0:
            keep = pltpu.make_async_copy(sendbuf.at[0], near.at[0, :, 0], zrecv.at[0])
            keep.start()
            continue
        zcopies[j] = pltpu.make_async_remote_copy(
            src_ref=sendbuf.at[j],
            dst_ref=near.at[j // 4, :, j % 4] if j < 8 else arr.at[0, :, j - 8],
            send_sem=zsend.at[j],
            recv_sem=zrecv.at[j],
            device_id=(peer_of(j, z, xl, c, y, xh, 1), h), device_id_type=MESH,
        )
        if j == 8:
            pl.semaphore_wait(barrier, 58)
        if j in (8, 1, 2, 3):
            zcopies[j].start()

    def wcopy(src, owner, to, n):
        slot = lax.rem(owner - lax.rem(to, 4) + 4, 4)
        return pltpu.make_async_remote_copy(
            src_ref=src, dst_ref=w_v.at[slot], send_sem=wsend.at[n], recv_sem=wrecv.at[n],
            device_id=(to, h), device_id_type=MESH,
        )

    w_mate = wcopy(w_out, g, core_mate, 0)
    w_far = wcopy(w_out, g, xl_mate, 1)
    w_pass = wcopy(w_v.at[2], lax.rem(g + 2, 4), core_mate, 2)

    scale = 1.4426950408889634 * 192 ** -0.5
    query_load.wait()
    query_f[0] = query_v[:, :128].astype(F32)
    query_f[1] = jnp.concatenate([query_v[:, 128:].astype(F32) * scale, jnp.zeros((1024, 64), F32)], axis=1)
    uk_load.wait()

    @pl.loop(0, 8)
    def _(two):
        cols = pl.ds(pl.multiple_of(two * 128, 128), 128)
        plain, rope = (
            jnp.concatenate([query_f[part, pl.ds(two * 2 + n, 64, stride=16), :] for n in range(2)], axis=0).astype(BF16)
            for part in range(2)
        )
        q_main[:, cols] = (scale * jnp.concatenate(
            [
                jnp.dot(plain[64 * n : 64 * (n + 1)], uk_v[two * 2 + n], preferred_element_type=F32)
                for n in range(2)
            ],
            axis=0,
        )).astype(BF16).T
        rope = rope.T
        q_low[:, cols] = rope
        q_high[:, cols] = jnp.concatenate([rope[64:], rope[:64]], axis=0)

    def fold(cols, s, values, first=False):
        top = jnp.max(s, axis=0, keepdims=True)
        if not first:
            before = m_s[:1, cols]
            top = jnp.maximum(top, before)
        p_ = jnp.exp2(s - top)
        total = jnp.sum(p_, axis=0, keepdims=True)
        mix = jnp.dot(values, p_.astype(BF16), preferred_element_type=F32)
        if not first:
            fade = jnp.exp2(before - top)
            total = total + l_s[:1, cols] * fade
            mix = mix + acc[:, cols] * fade
        acc[:, cols] = mix
        m_s[:1, cols] = top
        l_s[:1, cols] = total

    fresh_load.wait()
    new = fresh_v[...].reshape(64, 576)
    turned[:, :64] = new[:, :512].T
    ALL = pl.ds(0, 1024)
    s = jnp.dot(new[:, :512], q_main[...], preferred_element_type=F32)
    s = s + jnp.dot(new[:, 512:], q_low[:64, :], preferred_element_type=F32)
    token = lax.broadcasted_iota(jnp.int32, s.shape, 0)
    lane = lax.broadcasted_iota(jnp.int32, s.shape, 1)
    seen = (((lane >> 2) & 15) == (token >> 2)) & ((lane & 3) >= (token & 3))
    fold(ALL, jnp.where(seen, s, -jnp.inf), turned[:, :64], first=True)

    table_load.wait()
    length = table[32:33, :]
    whole = length >> 6
    position = lax.broadcasted_iota(jnp.int32, (32, 128), 0)
    full = jnp.where(position < whole, table[:32, :], -1)
    partial = jnp.max(jnp.where(position == whole, table[:32, :], -1), axis=0, keepdims=True)
    inside = lax.broadcasted_iota(jnp.int32, (64, 128), 0) < (length & 63)

    def fill_bias(n, page):
        count = jnp.sum(jnp.where(full == page, 1.0, 0.0), axis=0, keepdims=True)
        reads = count + jnp.where(inside & (partial == page), 1.0, 0.0)
        bias_v[64 * n : 64 * (n + 1), :] = jnp.where(reads > 0, jnp.log2(jnp.maximum(reads, 1.0)), -jnp.inf)

    def fill_pairs(n, offsets):
        for ab in range(2):
            for m, (dz, k) in enumerate(offsets):
                fill_bias(n + ab * len(offsets) + m, 48 + 2 * pool_at(dz, k, z, xl, c, -1) + ab)

    def biased(s, toks, width):
        b = bias_v[toks, :]
        return s + jnp.concatenate([b] * (width // 128), axis=1)

    def resident_chunk(n):
        for page in range(8 * n, 8 * n + 8):
            fill_bias(page, page)
        res_loads[n].wait()
        toks = pl.ds(512 * n, 512)
        turned[:, :512] = res_v[toks, :512].T
        s = jnp.dot(res_v[toks, :512], q_main[...], preferred_element_type=F32)
        s = s + jnp.dot(res_v[toks, 512:], q_low[:64, :], preferred_element_type=F32)
        fold(ALL, biased(s, toks, 1024), turned[:, :512])

    def arrived_chunk(held, first, count, tiles_of=(ALL,), after=None):
        half = 64 * count
        for ab in range(2):
            for j in range(4):
                turned[j * 128 : (j + 1) * 128, ab * half : (ab + 1) * half] = (
                    held[ab * 4 + j].reshape(half, 128).T
                )
        for cols in tiles_of:
            rope = held[8].reshape(half, 128)
            main = jnp.concatenate(
                [
                    jnp.concatenate([held[ab * 4 + j].reshape(half, 128) for j in range(4)], axis=1)
                    for ab in range(2)
                ],
                axis=0,
            )
            s = jnp.dot(main, q_main[:, cols], preferred_element_type=F32)
            s = s + jnp.concatenate(
                [jnp.dot(rope, q[:, cols], preferred_element_type=F32) for q in (q_low, q_high)], axis=0
            )
            fold(cols, biased(s, pl.ds(first, 2 * half), cols.size), turned[:, : 2 * half])
            if after is not None:
                after(cols)

    def near_chunk(n):
        fill_pairs(48 + 8 * n, DIRECT[4 * n : 4 * n + 4])
        arrived_chunk(near.at[n], 3072 + 512 * n, 4)

    def far_bias(rel):
        member = lax.rem(y + rel, 4)
        fill_pairs(64 + 12 * rel, [split_offset(m % 3, member, lax.rem(xh + m // 3, 2)) for m in range(6)])

    def far_chunk(rel, **how):
        arrived_chunk(arr.at[rel], 4096 + 768 * rel, 6, **how)

    def xcopy(i):
        return pltpu.make_async_remote_copy(
            src_ref=arr.at[0, :, i], dst_ref=arr.at[0, :, 3 + i],
            send_sem=xsend.at[i], recv_sem=xrecv.at[i], device_id=(p, across), device_id_type=MESH,
        )

    def ycopy(n, way, kind):
        landing = 2 if kind else (3 if way == 0 else 1)
        source = 0 if kind == 0 else (3 if way == 0 else 1)
        return pltpu.make_async_remote_copy(
            src_ref=arr.at[source, :, n], dst_ref=arr.at[landing, :, n],
            send_sem=ysend.at[way, kind, n], recv_sem=yrecv.at[way, kind, n],
            device_id=(p, up if way == 0 else down), device_id_type=MESH,
        )

    def own_step(n):
        if n < 3:
            zcopies[8 + n].wait_recv()
            xcopy(n).start()
        else:
            xcopy(n - 3).wait_recv()
        ycopy(n, 0, 0).start()
        ycopy(n, 1, 0).start()

    def pass_step(n):
        ycopy(n, 0, 0).wait_recv()
        ycopy(n, 1, 0).wait_recv()
        ycopy(n, n % 2, 1).start()

    zcopies[9].start()
    zcopies[10].start()
    resident_chunk(0)
    own_step(0)
    resident_chunk(1)
    own_step(1)
    own_step(2)
    for j in (4, 5, 6, 7):
        zcopies[j].start()
    w_mate.start()
    w_far.start()
    own_step(3)
    pass_step(0)
    own_step(4)
    own_step(5)
    pass_step(1)
    resident_chunk(2)
    pass_step(2)
    resident_chunk(3)
    pass_step(3)
    resident_chunk(4)
    pass_step(4)
    resident_chunk(5)
    keep.wait()
    for j in (1, 2, 3):
        zcopies[j].wait_recv()
    near_chunk(0)
    pass_step(5)
    for rel in range(4):
        far_bias(rel)
    far_chunk(0)
    for j in (4, 5, 6, 7):
        zcopies[j].wait_recv()
    near_chunk(1)
    far_chunk(3)
    far_chunk(1)
    w_far.wait_recv()
    w_pass.start()
    for n in range(6):
        ycopy(n, n % 2, 1).wait_recv()
    uv_load.wait()

    def hcopy(way, a, half):
        cols = pl.ds(1024 * half, 1024)
        src = 0 if a == 1 else 2 * (a - 1) - 1 + way
        dst = 7 if a == 4 else 2 * a - 1 + way
        return pltpu.make_async_remote_copy(
            src_ref=hbuf.at[src, :, cols], dst_ref=hbuf.at[dst, :, cols],
            send_sem=hsend.at[way, a - 1, half], recv_sem=hrecv.at[way, a - 1, half],
            device_id=(right if way == 0 else left, h), device_id_type=MESH,
        )

    def finish(cols):
        for two in range(cols.start // 128, (cols.start + cols.size) // 128):
            at = pl.ds(two * 128, 128)
            mixed = (acc[:, at] / l_s[:1, at]).astype(BF16).T
            for n in range(2):
                hbuf[0, :, two * 256 + n * 128 : two * 256 + (n + 1) * 128] = jnp.dot(
                    mixed[n * 64 : (n + 1) * 64], uv_v[two * 2 + n], preferred_element_type=F32
                ).astype(BF16)
        half = cols.start // 512
        hcopy(0, 1, half).start()
        hcopy(1, 1, half).start()

    far_chunk(2, tiles_of=(pl.ds(0, 512), pl.ds(512, 512)), after=finish)

    def tile_copy(slot, i, to_head):
        return pltpu.make_async_remote_copy(
            src_ref=tiles.at[slot, i], dst_ref=landed.at[h, g],
            send_sem=rsend.at[slot, i], recv_sem=rrecv.at[h, g],
            device_id=(z * 4 + lax.rem(g + i, 4), to_head), device_id_type=MESH,
        )

    def slot_head(slot):
        if slot == 0:
            return z
        if slot == 7:
            return lax.rem(z + 4, 8)
        a = (slot + 1) // 2
        return lax.rem(z + 8 - a, 8) if slot % 2 else lax.rem(z + a, 8)

    def multiply(first, count):
        lhs = hbuf[pl.ds(first, count)].reshape(64 * count, 2048)
        for i in range(4):
            part = lax.dot_general(lhs, w_v[i], NT, preferred_element_type=F32).astype(BF16)
            for n in range(count):
                slot = first + n
                to_head = slot_head(slot)
                tiles[slot, i] = part[64 * n : 64 * (n + 1)]
                copy = tile_copy(slot, i, to_head)
                if i == 0:
                    @pl.when(to_head != h)
                    def _(copy=copy):
                        copy.start()

                    @pl.when(to_head == h)
                    def _(slot=slot):
                        landed[h, g] = tiles[slot, 0]
                else:
                    copy.start()

    order = [(0, 0), (1, 0), (0, 1), (1, 1)]
    for a in range(1, 4):
        for way, half in order:
            hcopy(way, a, half).wait_recv()
            if a < 3 or way == half:
                hcopy(way, a + 1, half).start()
        if a == 1:
            w_load.wait()
            w_mate.wait_recv()
            w_pass.wait_recv()
            multiply(0, 3)
        else:
            multiply(2 * a - 1, 2)
    hcopy(0, 4, 0).wait_recv()
    hcopy(1, 4, 1).wait_recv()
    multiply(7, 1)

    for dh in range(8):
        for i in range(4):
            if dh or i:
                hh, gg = lax.rem(h + dh, 8), lax.rem(g + i, 4)
                pltpu.make_async_remote_copy(
                    src_ref=tiles.at[0, 0], dst_ref=landed.at[hh, gg],
                    send_sem=rsend.at[0, 0], recv_sem=rrecv.at[hh, gg],
                    device_id=(z * 4 + gg, hh), device_id_type=MESH,
                ).wait_recv()
    total = landed[0].astype(F32)
    for n in range(1, 8):
        total = total + landed[n].astype(F32)
    out[...] = total.astype(BF16)

    for j in range(1, 11):
        zcopies[j].wait_send()
    for i in range(3):
        xcopy(i).wait_send()
    for n in range(6):
        ycopy(n, 0, 0).wait_send()
        ycopy(n, 1, 0).wait_send()
        ycopy(n, n % 2, 1).wait_send()
    w_mate.wait_send()
    w_far.wait_send()
    w_pass.wait_send()
    for way, half in order:
        for a in range(1, 5):
            if a < 4 or way == half:
                hcopy(way, a, half).wait_send()
    for slot in range(8):
        to_head = slot_head(slot)
        for i in range(4):
            if i == 0:
                @pl.when(to_head != h)
                def _(slot=slot, to_head=to_head):
                    tile_copy(slot, 0, to_head).wait_send()
            else:
                tile_copy(slot, i, to_head).wait_send()


ANY = pl.BlockSpec(memory_space=pl.ANY)
VMEM = pl.BlockSpec(memory_space=pltpu.VMEM)
SMEM = pl.BlockSpec(memory_space=pltpu.SMEM)
DMA = pltpu.SemaphoreType.DMA


def per_device(
    span_cache, destination, resident, block_table, lengths, new_latent, query, w_uk, w_uv, w_out
):
    table = jnp.concatenate([block_table.T, lengths[None, :]], axis=0)
    table = jnp.broadcast_to(table[:, None, :, None], (33, 2, 16, 4)).reshape(33, 128)
    owners = jnp.pad(destination.reshape(1, 32), ((0, 6), (0, 96)))
    given = jnp.concatenate([table, owners], axis=0)
    out = pl.pallas_call(
        kernel,
        out_shape=jax.ShapeDtypeStruct((4, 64, 224), BF16),
        in_specs=[ANY] * 8,
        out_specs=VMEM,
        scratch_shapes=[
            pltpu.SMEM((8, 128), jnp.int32),
            pltpu.VMEM((40, 128), jnp.int32),
            pltpu.VMEM((32, 64, 576), BF16),
            pltpu.VMEM((3072, 576), BF16),
            pltpu.VMEM((16, 128, 512), BF16),
            pltpu.VMEM((16, 512, 128), BF16),
            pltpu.VMEM((16, 4, 576), BF16),
            pltpu.VMEM((1024, 192), BF16),
            pltpu.VMEM((2, 1024, 128), F32),
            pltpu.VMEM((7168, 128), F32),
            pltpu.VMEM((11, 9, 64, 128), BF16),
            pltpu.VMEM((2, 9, 4, 64, 128), BF16),
            pltpu.VMEM((4, 9, 6, 64, 128), BF16),
            pltpu.VMEM((512, 1024), BF16),
            pltpu.VMEM((128, 1024), BF16),
            pltpu.VMEM((128, 1024), BF16),
            pltpu.VMEM((512, 768), BF16),
            pltpu.VMEM((512, 1024), F32),
            pltpu.VMEM((8, 1024), F32),
            pltpu.VMEM((8, 1024), F32),
            pltpu.VMEM((4, 224, 2048), BF16),
            pltpu.VMEM((8, 64, 2048), BF16),
            pltpu.VMEM((8, 4, 64, 224), BF16),
            pltpu.VMEM((8, 4, 64, 224), BF16),
            DMA((8,)), DMA((6,)), DMA((11,)), DMA((11,)), DMA((3,)), DMA((3,)),
            DMA((2, 2, 6)), DMA((2, 2, 6)), DMA((3,)), DMA((3,)),
            DMA((2, 4, 2)), DMA((2, 4, 2)), DMA((8, 4)), DMA((8, 4)),
        ],
        compiler_params=pltpu.CompilerParams(
            collective_id=0, has_side_effects=True, vmem_limit_bytes=60 * 1024 * 1024
        ),
        name="handoff_attend_project",
    )(
        given, query.reshape(1024, 192), span_cache, resident.reshape(3072, 576), new_latent,
        w_uk, w_uv, w_out.T,
    )
    return out.reshape(64, 4, 224)


def solution(mesh):
    return jax.shard_map(
        per_device,
        mesh=mesh,
        in_specs=(
            P("pool", None, None),
            P("pool", None),
            P("pool", None, None),
            P("pool", None),
            P("pool"),
            P("pool", None, None),
            P("pool", None, "head", None),
            P("head", None, None),
            P("head", None, None),
            P("head", "pool"),
        ),
        out_specs=P("head", None, "pool"),
        check_vma=False,
    )
```
